256 devices in a mesh: inst: 32 (over y, x, z_lo), tp: 8 (over z_hi, core).
Axes of the slice: x: 4, y: 4, z: 8 (z_hi: 4, z_lo: 2; z = z_hi * 2 + z_lo), core: 2. Of those that a mesh axis runs over, the one named last changes fastest.
Arguments:
- queries: bfloat16 [256, 4, 8192], P('inst', None, 'tp'), may hold values from -12 to 12
- new_kv: bfloat16 [256, 4, 2048], P('inst', None, 'tp'), may hold values from -7.5 to 7.5
- pool: bfloat16 [2560, 128, 2048], P('inst', None, 'tp'), may hold values from -5 to 5
- page: int32 [256, 32], P('inst'), may hold values from 0 to 143, as said below
- lengths: int32 [256], P('inst'), may hold values from 1 to 4096, as said below
- outbox: int32 [32, 32, 2], P('inst'), may hold values from 0 to 79, as said below
- prefix_store: bfloat16 [131072, 2048], P(('inst', 'tp')), may hold values from -5 to 5
- owner: int32 [1], replicated, may hold values from 0 to 31
- flags: int32 [256], P('inst'), may hold values 0 or 1
Outputs:
- attention: bfloat16 [256, 4, 8192], P('inst', None, 'tp')
The draws below stay inside these ranges and needn't reach their ends.
Inputs may be any that keep to these rules, and one draw needn't show every extreme that they name: `page`: for request r, entries j < ceil(lengths[r] / 128) name distinct blocks of its instance's store: a value under 80 is a block of the instance's own pool that it sends to no one, and 80 + s * 2 + c is the c-th block that instance s sends it; each of the 64 received blocks is named exactly once. Later entries are arbitrary. On every instance the named blocks number at most 80, and exactly 80 on some instance. `lengths`: one request of every instance has exactly 4096 tokens. `outbox`: for each source instance the 64 entries are distinct blocks of its pool.
All inputs are finite; a program needn't handle non-finite values. No bound on the sum of `flags` on one device may be relied on, other than what follows from the above.
Results may differ from the reference program's by a relative error of at most 0.0028.
Values may be sent and summed in bfloat16 or wider, within the bound.
No kernel may reach another device: no remote copies, remote signals or barrier semaphores. Data moves between devices by JAX's collectives and lax.ppermute only.
A program may use at most 128 MiB of HBM per device.

```python
import jax
import jax.numpy as jnp
from jax import lax

H = 64
KVH = 8
HD = 128
BLK = 128
PLEN = 4096
STEPS = 4
MAXB = 32
CAP = 2
KEEP = 16
REQ = 8
POOL = 80
N_INST = 32


def routing(key):
    base = jax.random.fold_in(key, 7)
    big = jax.random.randint(jax.random.fold_in(base, 1), (), 0, N_INST, dtype=jnp.int32)
    keys = jax.random.split(jax.random.fold_in(base, 2), N_INST)
    incoming = N_INST * CAP
    units = REQ * (MAXB - 1)

    def one(inst_key, index):
        k_total, k_long, k_units, k_tail, k_pool, k_mix, k_fill = jax.random.split(inst_key, 7)
        total = incoming + jax.random.randint(k_total, (), KEEP // 2, KEEP + 1, dtype=jnp.int32)
        total = jnp.where(index == big, POOL, total)
        longest = jax.random.randint(k_long, (), 0, REQ, dtype=jnp.int32)
        owner_of = jnp.repeat(jnp.arange(REQ, dtype=jnp.int32), MAXB - 1)
        within = jnp.tile(jnp.arange(MAXB - 1, dtype=jnp.int32), REQ)
        shuffled = jax.random.permutation(k_units, units).astype(jnp.int32)
        score = jnp.where(owner_of == longest, within - MAXB, shuffled)
        sorted_units = jnp.argsort(score, stable=True).astype(jnp.int32)
        rank = jnp.zeros((units,), jnp.int32).at[sorted_units].set(jnp.arange(units, dtype=jnp.int32))
        picked = rank < total - REQ
        hits = (owner_of[:, None] == jnp.arange(REQ, dtype=jnp.int32)[None, :]) & picked[:, None]
        blocks = 1 + jnp.sum(hits.astype(jnp.int32), axis=0).astype(jnp.int32)
        tail = jax.random.randint(k_tail, (REQ,), 1, BLK + 1, dtype=jnp.int32)
        tail = jnp.where(jnp.arange(REQ, dtype=jnp.int32) == longest, BLK, tail)
        lens = (blocks - 1) * BLK + tail
        pool_order = jax.random.permutation(k_pool, POOL).astype(jnp.int32)
        outgoing = pool_order[:incoming].reshape(N_INST, CAP)
        kept = pool_order[incoming:]
        candidates = jnp.concatenate([POOL + jnp.arange(incoming, dtype=jnp.int32), kept])
        slots = jnp.arange(POOL, dtype=jnp.int32)
        mixing = jnp.where(slots < total, jax.random.permutation(k_mix, POOL).astype(jnp.int32), POOL + slots)
        arranged = candidates[jnp.argsort(mixing, stable=True)]
        live = (jnp.arange(MAXB, dtype=jnp.int32)[None, :] < blocks[:, None]).reshape(-1)
        place = jnp.cumsum(live.astype(jnp.int32)).astype(jnp.int32) - 1
        filler = jax.random.randint(k_fill, (REQ * MAXB,), 0, POOL + incoming, dtype=jnp.int32)
        pages = jnp.where(live, arranged[jnp.clip(place, 0, POOL - 1)], filler).reshape(REQ, MAXB)
        return (pages, lens, outgoing)
    pages, lens, outgoing = jax.vmap(one)(keys, jnp.arange(N_INST, dtype=jnp.int32))
    return (pages.reshape(N_INST * REQ, MAXB).astype(jnp.int32), lens.reshape(-1).astype(jnp.int32), outgoing.astype(jnp.int32))


def draw_page(key, part):
    return routing(key)[0]


def draw_lengths(key, part):
    return routing(key)[1]


def draw_outbox(key, part):
    return routing(key)[2]


def draw_pool(key, part):
    key = jax.random.fold_in(key, 1)
    shape = (N_INST * POOL * BLK, KVH, 2, HD)
    values = jnp.clip(jax.random.normal(key, shape, jnp.float32), -5.0, 5.0)
    return values.reshape(N_INST * POOL, BLK, KVH * 2 * HD).astype(jnp.bfloat16)


def draw_prefix_store(key, part):
    key = jax.random.fold_in(key, 2)
    shape = (N_INST * PLEN, KVH, 2, HD)
    values = jnp.clip(jax.random.normal(key, shape, jnp.float32), -5.0, 5.0)
    return values.reshape(N_INST * PLEN, KVH * 2 * HD).astype(jnp.bfloat16)


def draw_queries(key, part):
    key = jax.random.fold_in(key, 3)
    group = H // KVH
    shape = (N_INST * REQ, STEPS, KVH, group, HD)
    values = jnp.clip(3.0 * jax.random.normal(key, shape, jnp.float32), -12.0, 12.0)
    return values.reshape(N_INST * REQ, STEPS, H * HD).astype(jnp.bfloat16)


def with_ends(values, rng, least, largest):
    longest = values.shape.index(max(values.shape))
    spots = []
    for shift in (0, 1):
        where = [jax.random.randint(jax.random.fold_in(rng, axis), (), 0, length) for axis, length in enumerate(values.shape)]
        where[longest] = (where[longest] + shift) % values.shape[longest]
        spots.append(tuple(where))
    return values.at[spots[0]].set(least).at[spots[1]].set(largest)


def shard_levels(own_key, dims, pieces, low, top_value):
    loudness, own = 1.0, jax.random.fold_in(own_key, 6)
    for position, blocks in pieces:
        steps = jnp.exp(jax.random.uniform(jax.random.fold_in(own, position), (blocks,), jnp.float32, low / len(pieces), top_value / len(pieces)))
        loudness = loudness * jnp.repeat(steps, dims[position] // blocks).reshape([-1 if axis == position else 1 for axis in range(len(dims))])
    return loudness


def normal_values(own_key, dims, deviation, limit, shards=(), kind=jnp.bfloat16):
    values = deviation * jax.random.normal(own_key, dims, jnp.float32)
    if shards:
        values = values * shard_levels(own_key, dims, shards, -0.22, 0.18)
    return jnp.clip(values, -limit, limit).astype(kind)


def setup_inputs(seed: int = 0) -> dict:
    key_of = jax.random.split(jax.random.key(seed), 10)
    return {
        "queries": draw_queries(jax.random.fold_in(key_of[9], 71), 0),
        "new_kv": normal_values(key_of[1], (N_INST * REQ, STEPS, KVH * 2 * HD), 1.5, 7.5, ((0, 32), (2, 8))),
        "pool": draw_pool(jax.random.fold_in(key_of[9], 71), 0),
        "page": draw_page(jax.random.fold_in(key_of[9], 71), 0),
        "lengths": draw_lengths(jax.random.fold_in(key_of[9], 71), 0),
        "outbox": draw_outbox(jax.random.fold_in(key_of[9], 71), 0),
        "prefix_store": draw_prefix_store(jax.random.fold_in(key_of[9], 71), 0),
        "owner": jax.random.randint(key_of[7], (1,), 0, N_INST).astype(jnp.int32),
        "flags": with_ends((jax.random.randint(key_of[8], (N_INST * REQ,), 0, 4) < 3).astype(jnp.int32), jax.random.fold_in(key_of[8], 1), 0, 1),
    }


NEG = -1.0e30


def part_stats(scores, valid):
    masked = jnp.where(valid, scores, -jnp.inf)
    top = jnp.max(masked, axis=-1)
    top = jnp.where(jnp.any(valid, axis=-1), top, NEG)
    weights = jnp.where(valid, jnp.exp(scores - top[..., None]), 0.0).astype(jnp.bfloat16)
    total = jnp.sum(weights.astype(jnp.float32), axis=-1)
    return top, weights, total


def combine_parts(parts):
    peak = parts[0][0].max(axis=1)
    for entry in parts[1:]:
        peak = jnp.maximum(peak, entry[0].max(axis=1))
    numer = jnp.zeros(parts[0][2].shape[:1] + parts[0][2].shape[2:], jnp.float32)
    denom = jnp.zeros(peak.shape, jnp.float32)
    for top, total, out in parts:
        factor = jnp.exp(top - peak[:, None])
        numer = numer + jnp.sum(factor[..., None] * out, axis=1)
        denom = denom + jnp.sum(factor * total, axis=1)
    return numer / denom[..., None]


def reference(queries, new_kv, pool, page, lengths, outbox, prefix_store, owner, flags):
    scale = HD ** -0.5
    group = H // KVH
    start = owner[0].astype(jnp.int32) * PLEN
    prefix = lax.dynamic_slice_in_dim(prefix_store, start, PLEN, 0)
    prefix = prefix.reshape(PLEN // BLK, BLK, KVH, 2, HD).astype(jnp.float32)
    block_base = jnp.arange(N_INST, dtype=jnp.int32)[:, None] * POOL

    def one(index):
        first = index * REQ
        q_rows = lax.dynamic_slice_in_dim(queries, first, REQ, 0).reshape(REQ, STEPS, KVH, group, HD).astype(jnp.float32)
        fresh = lax.dynamic_slice_in_dim(new_kv, first, REQ, 0).reshape(REQ, STEPS, KVH, 2, HD).astype(jnp.float32)
        own = lax.dynamic_slice_in_dim(pool, index * POOL, POOL, 0)
        sent = lax.dynamic_index_in_dim(outbox, index, 1, keepdims=False)
        arrived = pool[(block_base + sent).reshape(-1)]
        store = jnp.concatenate([own, arrived], axis=0)
        pages = lax.dynamic_slice_in_dim(page, first, REQ, 0)
        lens = lax.dynamic_slice_in_dim(lengths, first, REQ, 0)
        marks = lax.dynamic_slice_in_dim(flags, first, REQ, 0)
        blocks = store[pages].reshape(REQ, MAXB, BLK, KVH, 2, HD).astype(jnp.float32)
        counts = jnp.clip(lens[:, None] - jnp.arange(MAXB, dtype=jnp.int32)[None, :] * BLK, 0, BLK)

        ctx_scores = jnp.einsum("rsngd,rjtnd->rjsngt", q_rows, blocks[:, :, :, :, 0]) * scale
        place = jnp.arange(BLK, dtype=jnp.int32)
        ctx_valid = place[None, None, :] < counts[:, :, None]
        ctx_valid = jnp.broadcast_to(ctx_valid[:, :, None, None, None, :], ctx_scores.shape)
        ctx_top, ctx_weights, ctx_total = part_stats(ctx_scores, ctx_valid)
        ctx_out = jnp.einsum("rjsngt,rjtnd->rjsngd", ctx_weights.astype(jnp.float32), blocks[:, :, :, :, 1])

        pre_scores = jnp.einsum("rsngd,ptnd->rpsngt", q_rows, prefix[:, :, :, 0]) * scale
        pre_valid = jnp.broadcast_to((marks == 1)[:, None, None, None, None, None], pre_scores.shape)
        pre_top, pre_weights, pre_total = part_stats(pre_scores, pre_valid)
        pre_out = jnp.einsum("rpsngt,ptnd->rpsngd", pre_weights.astype(jnp.float32), prefix[:, :, :, 1])

        new_scores = jnp.einsum("rsngd,rund->rsngu", q_rows, fresh[:, :, :, 0]) * scale
        order = jnp.arange(STEPS, dtype=jnp.int32)
        new_valid = jnp.broadcast_to((order[None, :] <= order[:, None])[None, :, None, None, :], new_scores.shape)
        new_top, new_weights, new_total = part_stats(new_scores, new_valid)
        new_out = jnp.einsum("rsngu,rund->rsngd", new_weights.astype(jnp.float32), fresh[:, :, :, 1])

        result = combine_parts([(pre_top, pre_total, pre_out), (ctx_top, ctx_total, ctx_out),
                                (new_top[:, None], new_total[:, None], new_out[:, None])])
        return result.astype(jnp.bfloat16).reshape(REQ, STEPS, H * HD)

    outputs = lax.map(one, jnp.arange(N_INST, dtype=jnp.int32))
    return outputs.reshape(N_INST * REQ, STEPS, H * HD)
```

```python
import functools

import jax
import jax.numpy as jnp
from jax import lax
from jax.experimental import pallas as pl
from jax.experimental.pallas import tpu as pltpu
from jax.sharding import PartitionSpec as P

HD = 128
BLK = 128
CAP = 2
KEPT = 16
NEG = -1e30
F32 = jnp.float32
BF16 = jnp.bfloat16

VMEM = pl.BlockSpec(memory_space=pltpu.VMEM)
SMEM = pl.BlockSpec(memory_space=pltpu.SMEM)


def params():
    return pltpu.CompilerParams(vmem_limit_bytes=40 * 1024 * 1024)


def cost(us):
    return pl.CostEstimate(flops=0, bytes_accessed=int(us * 3.0e6), transcendentals=0)


def dot_nt(a, b):
    return lax.dot_general(a, b, (((1,), (1,)), ((), ())), preferred_element_type=F32)


def dot_nn(a, b):
    return lax.dot_general(a, b, (((1,), (0,)), ((), ())), preferred_element_type=F32)


def with_ones(values):
    return jnp.concatenate([values, jnp.ones_like(values)], axis=1)


def block_partial(q, keys, values, valid):
    scores = dot_nt(q, keys) * (HD ** -0.5)
    if valid is not None:
        scores = jnp.where(valid, scores, NEG)
    top = jnp.max(scores, axis=-1, keepdims=True)
    weights = jnp.exp(scores - top)
    if valid is not None:
        weights = jnp.where(valid, weights, 0.0)
    both = dot_nn(weights.astype(BF16), with_ones(values))
    return top, both[:, HD:], both[:, :HD]


def prep_kernel(pool_size, page, lens, q, pay, local, slot_req, counts):
    n = pay.shape[0]
    rows = q.shape[1]
    for k in range(KEPT):
        for field in range(3):
            local[field, k] = 0

    def request(r, kept):
        length = lens[r]

        def block(j, kept):
            b = page[r, j]
            valid = jnp.minimum(length - j * BLK, BLK)
            away = b >= pool_size

            @pl.when(away)
            def _():
                slot = b - pool_size
                slot_req[slot] = r
                counts[slot] = valid
                at = pl.multiple_of(lax.bitwise_and(slot, 1) * rows, rows)
                pay[lax.shift_right_logical(slot, 1), pl.ds(at, rows), :] = q[r]

            @pl.when(jnp.logical_not(away))
            def _():
                local[0, kept] = b
                local[1, kept] = r
                local[2, kept] = valid

            return kept + jnp.where(away, 0, 1)

        return lax.fori_loop(0, lax.shift_right_logical(length + BLK - 1, 7), block, kept)

    lax.fori_loop(0, q.shape[0], request, 0)
    upper = lax.broadcasted_iota(jnp.int32, (16, HD), 0) < 8

    def mark(d, carry):
        tile = jnp.where(upper, counts[2 * d], counts[2 * d + 1])
        pay[d, CAP * rows : CAP * rows + 16, :] = tile.astype(F32).astype(BF16)
        return carry

    lax.fori_loop(0, n, mark, 0)


def prep(page, lengths, q, pool_size, n):
    req, rows, _ = q.shape
    return pl.pallas_call(
        functools.partial(prep_kernel, pool_size),
        out_shape=(
            jax.ShapeDtypeStruct((n, CAP * rows + 16, HD), BF16),
            jax.ShapeDtypeStruct((3, KEPT), jnp.int32),
            jax.ShapeDtypeStruct((n * CAP,), jnp.int32),
        ),
        in_specs=[SMEM, SMEM, VMEM],
        out_specs=(VMEM, SMEM, SMEM),
        scratch_shapes=[pltpu.SMEM((n * CAP,), jnp.int32)],
        compiler_params=params(),
        cost_estimate=cost(4),
        name="prep",
    )(page, lengths, q)


def remote_kernel(outbox, pool, pay, ret):
    n = pay.shape[0]
    rows = (pay.shape[1] - 16) // CAP
    each = BLK // rows
    lane = lax.broadcasted_iota(jnp.int32, (rows, BLK), 1)

    def group(g, carry):
        stats = []
        for i in range(each):
            d = g * each + i
            marks = pay[d, CAP * rows : CAP * rows + 16, :].astype(F32)
            stat = jnp.zeros((rows, BLK), F32)
            for c in range(CAP):
                kv = pool[outbox[d * CAP + c]]
                valid = lane < marks[8 * c : 8 * c + 1, :].astype(jnp.int32)
                top, total, out = block_partial(
                    pay[d, c * rows : (c + 1) * rows, :], kv[:, :HD], kv[:, HD:], valid
                )
                ret[d, c * rows : (c + 1) * rows, :] = out
                stat = jnp.where(lane == 2 * c, top, stat)
                stat = jnp.where(lane == 2 * c + 1, total, stat)
            stats.append(stat)
        turned = jnp.concatenate(stats, axis=0).T[:8]
        for i in range(each):
            ret[g * each + i, CAP * rows : CAP * rows + 8, :] = turned
        return carry

    lax.fori_loop(0, n // each, group, 0)


def remote_partials(outbox, pool, pay):
    n, height, _ = pay.shape
    return pl.pallas_call(
        remote_kernel,
        out_shape=jax.ShapeDtypeStruct((n, height - 8, HD), F32),
        in_specs=[SMEM, VMEM, VMEM],
        out_specs=VMEM,
        compiler_params=params(),
        cost_estimate=cost(8),
        name="remote_partials",
    )(outbox, pool, pay)


def local_kernel(local, pool, q, fresh, out_o, out_m, out_l):
    req, rows, _ = q.shape
    steps = rows // 8
    keys = fresh.shape[1]
    step = lax.broadcasted_iota(jnp.int32, (rows, keys), 0) // 8
    place = lax.broadcasted_iota(jnp.int32, (rows, keys), 1)
    causal = (place <= step) & (place < steps)
    for r in range(req):
        top, total, out = block_partial(q[r], fresh[r, :, :HD], fresh[r, :, HD:], causal)
        out_o[r] = out
        out_l[r] = total
        out_m[r] = jnp.broadcast_to(top, (rows, HD))
    lane = lax.broadcasted_iota(jnp.int32, (rows, BLK), 1)

    def batch(g, carry):
        found = []
        for i in range(8):
            k = g * 8 + i
            kv = pool[local[0, k]]
            found.append(
                block_partial(q[local[1, k]], kv[:, :HD], kv[:, HD:], lane < local[2, k])
            )
        for i in range(8):
            r = local[1, g * 8 + i]
            top, total, out = found[i]
            old = out_m[r]
            new = jnp.maximum(old, top)
            keep, add = jnp.exp(old - new), jnp.exp(top - new)
            out_m[r] = new
            out_l[r] = out_l[r] * keep + total * add
            out_o[r] = out_o[r] * keep + out * add
        return carry

    lax.fori_loop(0, KEPT // 8, batch, 0)


def local_partials(local, pool, q, fresh):
    one = jax.ShapeDtypeStruct(q.shape, F32)
    return pl.pallas_call(
        local_kernel,
        out_shape=(one, one, one),
        in_specs=[SMEM, VMEM, VMEM, VMEM],
        out_specs=(VMEM, VMEM, VMEM),
        compiler_params=params(),
        cost_estimate=cost(6),
        name="local_partials",
    )(local, pool, q, fresh)


def prefix_kernel(q, kv, out_o, out_m, out_l):
    pieces, shares, tokens, _ = kv.shape
    each = BLK // tokens
    out_o[...] = jnp.zeros_like(out_o)
    out_l[...] = jnp.zeros_like(out_l)
    out_m[...] = jnp.full_like(out_m, NEG)

    def share(t, carry):
        found = []
        for b in range(pieces // each):
            block = kv[b * each : (b + 1) * each, t].reshape(BLK, 2 * HD)
            found.append(block_partial(q[...], block[:, :HD], block[:, HD:], None))
        old = out_m[...]
        new = old
        for top, _, _ in found:
            new = jnp.maximum(new, top)
        keep = jnp.exp(old - new)
        acc_l, acc_o = out_l[...] * keep, out_o[...] * keep
        for top, total, out in found:
            add = jnp.exp(top - new)
            acc_l = acc_l + total * add
            acc_o = acc_o + out * add
        out_m[...] = new
        out_l[...] = acc_l
        out_o[...] = acc_o
        return carry

    lax.fori_loop(0, shares, share, 0)


def prefix_partials(q, kv):
    one = jax.ShapeDtypeStruct(q.shape, F32)
    return pl.pallas_call(
        prefix_kernel,
        out_shape=(one, one, one),
        in_specs=[VMEM, VMEM],
        out_specs=(VMEM, VMEM, VMEM),
        compiler_params=params(),
        cost_estimate=cost(8),
        name="prefix_partials",
    )(q, kv)


def final_kernel(me, slot_req, flags, ret, lo, lm, ll, po, pm, plen, out, top, total, acc, turned):
    req, rows, _ = lo.shape
    n = ret.shape[0]
    batch = min(16, n)
    body = CAP * rows
    for r in range(req):
        use = flags[r] == 1
        past = jnp.where(use, pm[r], NEG)
        top[r] = jnp.maximum(lm[r], past)
    for g in range(n // batch):
        tiles = ret[g * batch : (g + 1) * batch, body : body + 8, :]
        turned[g] = tiles.reshape(batch * 8, BLK).T
    mine = pl.multiple_of(lax.rem(me[0], BLK // rows) * rows, rows)
    for g in range(n // batch):
        stats = turned[g, pl.ds(mine, rows), :]
        for i in range(batch):
            for c in range(CAP):
                r = slot_req[(g * batch + i) * CAP + c]
                col = 8 * i + 2 * c
                top[r] = jnp.maximum(top[r], stats[:, col : col + 1])
    for r in range(req):
        use = flags[r] == 1
        peak = top[r]
        past = jnp.exp(jnp.where(use, pm[r], NEG) - peak)
        here = jnp.exp(lm[r] - peak)
        total[r] = ll[r] * here + plen[r] * past
        acc[r] = lo[r] * here + po[r] * past
    for g in range(n // batch):
        stats = turned[g, pl.ds(mine, rows), :]
        for i in range(batch):
            for c in range(CAP):
                s = g * batch + i
                r = slot_req[s * CAP + c]
                col = 8 * i + 2 * c
                factor = jnp.exp(stats[:, col : col + 1] - top[r])
                total[r] += stats[:, col + 1 : col + 2] * factor
                acc[r] += ret[s, c * rows : (c + 1) * rows, :] * factor
    for r in range(req):
        out[r] = (acc[r] / total[r]).astype(BF16)


def final(me, slot_req, flags, ret, here, past):
    req, rows, _ = here[0].shape
    n = ret.shape[0]
    batch = min(16, n)
    whole = pltpu.VMEM((req, rows, HD), F32)
    return pl.pallas_call(
        final_kernel,
        out_shape=jax.ShapeDtypeStruct((req, rows, HD), BF16),
        in_specs=[SMEM, SMEM, SMEM] + [VMEM] * 7,
        out_specs=VMEM,
        scratch_shapes=[whole, whole, whole, pltpu.VMEM((n // batch, BLK, batch * 8), F32)],
        compiler_params=params(),
        cost_estimate=cost(4),
        name="final",
    )(me, slot_req, flags, ret, *here, *past)


def after(value, other):
    return lax.optimization_barrier((value, other))[0]


def per_device(queries, new_kv, pool, page, lengths, outbox, prefix_store, owner, flags):
    req, steps, width = queries.shape
    pool_size = pool.shape[0]
    group = width // HD
    rows = steps * group
    n = lax.axis_size("inst")
    shares = lax.axis_size("tp")
    me = lax.axis_index("inst").astype(jnp.int32).reshape(1)
    held, wide = prefix_store.shape
    tokens = held // n

    scattered = lax.all_to_all(
        prefix_store.reshape(n, tokens, wide), "inst", split_axis=0, concat_axis=0, tiled=True
    )
    q = queries.reshape(req, rows, HD)
    pay, local, slot_req = prep(page, lengths, q, pool_size, n)
    asked = lax.all_to_all(pay, "inst", split_axis=0, concat_axis=0, tiled=True)
    piece = lax.dynamic_index_in_dim(scattered, owner[0], 0, keepdims=False)
    piece = piece.reshape(tokens, shares, wide // shares).transpose(1, 0, 2)
    piece = lax.all_to_all(
        after(piece, asked), "tp", split_axis=0, concat_axis=0, tiled=True
    )
    ret = remote_partials(outbox.reshape(-1), pool, asked)
    fresh = jnp.pad(new_kv, ((0, 0), (0, 16 - steps), (0, 0)))
    here = local_partials(local, pool, q, fresh)
    prefix = lax.all_to_all(
        jnp.broadcast_to(piece[None], (n,) + piece.shape),
        "inst",
        split_axis=0,
        concat_axis=0,
        tiled=True,
    )
    back = lax.all_to_all(after(ret, prefix), "inst", split_axis=0, concat_axis=0, tiled=True)
    past = prefix_partials(q.reshape(req * rows, HD), prefix)
    past = [x.reshape(req, rows, HD) for x in past]
    out = final(me, slot_req, flags, back, here, past)
    return out.reshape(req, steps, width)


def solution(mesh):
    placed = (
        P("inst", None, "tp"),
        P("inst", None, "tp"),
        P("inst", None, "tp"),
        P("inst", None),
        P("inst"),
        P("inst", None, None),
        P(("inst", "tp"), None),
        P(),
        P("inst"),
    )
    return jax.shard_map(
        per_device, mesh=mesh, in_specs=placed, out_specs=P("inst", None, "tp"), check_vma=False
    )
```

```python
import functools

import jax
import jax.numpy as jnp
from jax import lax
from jax.experimental import pallas as pl
from jax.experimental.pallas import tpu as pltpu
from jax.sharding import PartitionSpec as P

HD = 128
BLK = 128
CAP = 2
KEPT = 16
NEG = -1e30
XS = 4
ZS = 2
F32 = jnp.float32
BF16 = jnp.bfloat16

VMEM = pl.BlockSpec(memory_space=pltpu.VMEM)
SMEM = pl.BlockSpec(memory_space=pltpu.SMEM)


def params():
    return pltpu.CompilerParams(vmem_limit_bytes=16 * 1024 * 1024)


def cost(us):
    return pl.CostEstimate(flops=0, bytes_accessed=int(us * 3.0e6), transcendentals=0)


def dot_nt(a, b):
    return lax.dot_general(a, b, (((1,), (1,)), ((), ())), preferred_element_type=F32)


def dot_nn(a, b):
    return lax.dot_general(a, b, (((1,), (0,)), ((), ())), preferred_element_type=F32)


def with_ones(values):
    return jnp.concatenate([values, jnp.ones_like(values)], axis=1)


def batch_partials(jobs):
    rows = jobs[0][0].shape[0]
    scores = jnp.concatenate([dot_nt(q, keys) for q, keys, _, _ in jobs], axis=0) * (HD ** -0.5)
    masked = jobs[0][3] is not None
    if masked:
        valid = jnp.concatenate([job[3] for job in jobs], axis=0)
        scores = jnp.where(valid, scores, NEG)
    top = jnp.max(scores, axis=-1, keepdims=True)
    weights = jnp.exp(scores - top)
    if masked:
        weights = jnp.where(valid, weights, 0.0)
    weights = weights.astype(BF16)
    found = []
    for i, (_, _, values, _) in enumerate(jobs):
        both = dot_nn(weights[i * rows : (i + 1) * rows], with_ones(values))
        found.append((top[i * rows : (i + 1) * rows], both[:, HD:], both[:, :HD]))
    return found


def prep_kernel(pool_size, page, lens, local, slot_req, counts):
    for k in range(KEPT):
        for field in range(3):
            local[field, k] = 0

    def request(r, kept):
        length = lens[r]

        def block(j, kept):
            b = page[r, j]
            valid = jnp.minimum(length - j * BLK, BLK)
            away = b >= pool_size

            @pl.when(away)
            def _():
                slot_req[b - pool_size] = r
                counts[b - pool_size] = valid

            @pl.when(jnp.logical_not(away))
            def _():
                local[0, kept] = b
                local[1, kept] = r
                local[2, kept] = valid

            return kept + jnp.where(away, 0, 1)

        return lax.fori_loop(0, lax.shift_right_logical(length + BLK - 1, 7), block, kept)

    lax.fori_loop(0, lens.shape[0], request, 0)


def prep(page, lengths, pool_size, slots):
    return pl.pallas_call(
        functools.partial(prep_kernel, pool_size),
        out_shape=(
            jax.ShapeDtypeStruct((3, KEPT), jnp.int32),
            jax.ShapeDtypeStruct((slots,), jnp.int32),
            jax.ShapeDtypeStruct((slots,), jnp.int32),
        ),
        in_specs=[SMEM, SMEM],
        out_specs=(SMEM, SMEM, SMEM),
        compiler_params=params(),
        cost_estimate=cost(3),
        name="prep",
    )(page, lengths)


def pack_kernel(spots, slot_req, counts, hold, q, c0, c1, c2, c3, pay):
    rows = q.shape[1]
    body = CAP * rows
    upper = lax.broadcasted_iota(jnp.int32, (16, HD), 0) < 8
    tokens = c0.shape[0] // len(spots)
    for d in range(len(spots)):
        for c in range(CAP):
            pay[d, c * rows : (c + 1) * rows, :] = q[slot_req[CAP * d + c]]
        tile = jnp.where(upper, counts[CAP * d], counts[CAP * d + 1])
        pay[d, body : body + 16, :] = tile.astype(F32).astype(BF16)
    for k, source in enumerate((c0, c1, c2, c3)):

        @pl.when(hold[0] == k)
        def _():
            for d, spot in enumerate(spots):
                for j in range(source.shape[1] // HD):
                    at = body + 16 + j * tokens
                    pay[d, at : at + tokens, :] = source[
                        spot * tokens : (spot + 1) * tokens, j * HD : (j + 1) * HD
                    ]


def pack(spots, slot_req, counts, hold, q, columns):
    n = len(spots)
    rows = q.shape[1]
    held, wide = columns[0].shape
    height = CAP * rows + 16 + (wide // HD) * (held // n)
    return pl.pallas_call(
        functools.partial(pack_kernel, spots),
        out_shape=jax.ShapeDtypeStruct((n, height, HD), BF16),
        in_specs=[SMEM, SMEM, SMEM] + [VMEM] * 5,
        out_specs=VMEM,
        compiler_params=params(),
        cost_estimate=cost(1.5),
        name="pack",
    )(slot_req, counts, hold, q, *columns)


def remote_kernel(outbox, pool, pay, ret):
    n = pay.shape[0]
    rows = (ret.shape[1] - 8) // CAP
    each = BLK // rows
    lane = lax.broadcasted_iota(jnp.int32, (rows, BLK), 1)

    def group(g, carry):
        jobs = []
        for i in range(each):
            d = g * each + i
            marks = pay[d, CAP * rows : CAP * rows + 16, :].astype(F32).astype(jnp.int32)
            for c in range(CAP):
                kv = pool[outbox[d * CAP + c]]
                valid = lane < marks[8 * c : 8 * c + 1, :]
                jobs.append((pay[d, c * rows : (c + 1) * rows, :], kv[:, :HD], kv[:, HD:], valid))
        found = batch_partials(jobs)
        stats = []
        for i in range(each):
            stat = jnp.zeros((rows, BLK), F32)
            for c in range(CAP):
                top, total, out = found[i * CAP + c]
                ret[g * each + i, c * rows : (c + 1) * rows, :] = out
                stat = jnp.where(lane == 2 * c, top, stat)
                stat = jnp.where(lane == 2 * c + 1, total, stat)
            stats.append(stat)
        turned = jnp.concatenate(stats, axis=0).T[:8]
        for i in range(each):
            ret[g * each + i, CAP * rows : CAP * rows + 8, :] = turned
        return carry

    lax.fori_loop(0, n // each, group, 0)


def remote_partials(outbox, pool, pay, rows):
    n = pay.shape[0]
    return pl.pallas_call(
        remote_kernel,
        out_shape=jax.ShapeDtypeStruct((n, CAP * rows + 8, HD), F32),
        in_specs=[SMEM, VMEM, VMEM],
        out_specs=VMEM,
        compiler_params=params(),
        cost_estimate=cost(8),
        name="remote_partials",
    )(outbox, pool, pay)


def local_kernel(local, pool, q, fresh, out_o, out_m, out_l):
    req, rows, _ = q.shape
    steps = rows // 8
    keys = fresh.shape[1]
    step = lax.broadcasted_iota(jnp.int32, (rows, keys), 0) // 8
    place = lax.broadcasted_iota(jnp.int32, (rows, keys), 1)
    causal = (place <= step) & (place < steps)
    found = batch_partials([(q[r], fresh[r, :, :HD], fresh[r, :, HD:], causal) for r in range(req)])
    for r, (top, total, out) in enumerate(found):
        out_o[r] = out
        out_l[r] = total
        out_m[r] = jnp.broadcast_to(top, (rows, HD))
    lane = lax.broadcasted_iota(jnp.int32, (rows, BLK), 1)

    def batch(g, carry):
        jobs = []
        for i in range(8):
            k = g * 8 + i
            kv = pool[local[0, k]]
            jobs.append((q[local[1, k]], kv[:, :HD], kv[:, HD:], lane < local[2, k]))
        found = batch_partials(jobs)
        for i in range(8):
            r = local[1, g * 8 + i]
            top, total, out = found[i]
            old = out_m[r]
            new = jnp.maximum(old, top)
            keep, add = jnp.exp(old - new), jnp.exp(top - new)
            out_m[r] = new
            out_l[r] = out_l[r] * keep + total * add
            out_o[r] = out_o[r] * keep + out * add
        return carry

    lax.fori_loop(0, KEPT // 8, batch, 0)


def local_partials(local, pool, q, fresh):
    one = jax.ShapeDtypeStruct(q.shape, F32)
    return pl.pallas_call(
        local_kernel,
        out_shape=(one, one, one),
        in_specs=[SMEM, VMEM, VMEM, VMEM],
        out_specs=(VMEM, VMEM, VMEM),
        compiler_params=params(),
        cost_estimate=cost(6),
        name="local_partials",
    )(local, pool, q, fresh)


def prefix_kernel(q0, q1, q2, q3, kv, p0, p1, p2, p3, q, out_o, out_m, out_l):
    pieces, shares, double, _ = kv.shape
    tokens = double // 2
    part = q0.shape[0]
    for s, source in enumerate((q0, q1, q2, q3)):
        q[s * part : (s + 1) * part, :] = source[...]
    out_o[...] = jnp.zeros_like(out_o)
    out_l[...] = jnp.zeros_like(out_l)
    out_m[...] = jnp.full_like(out_m, NEG)

    def pair(t, carry):
        jobs = []
        for b in range(2):
            keys = kv[:, 2 * t + b, :tokens].reshape(BLK, HD)
            values = kv[:, 2 * t + b, tokens:].reshape(BLK, HD)
            jobs.append((q[...], keys, values, None))
        found = batch_partials(jobs)
        old = out_m[...]
        new = jnp.maximum(jnp.maximum(old, found[0][0]), found[1][0])
        keep = jnp.exp(old - new)
        acc_l, acc_o = out_l[...] * keep, out_o[...] * keep
        for top, total, out in found:
            add = jnp.exp(top - new)
            acc_l = acc_l + total * add
            acc_o = acc_o + out * add
        out_m[...] = new
        out_l[...] = acc_l
        out_o[...] = acc_o
        return carry

    lax.fori_loop(0, shares // 2, pair, 0)
    lane = lax.broadcasted_iota(jnp.int32, (BLK, HD), 1)
    for s, target in enumerate((p0, p1, p2, p3)):
        target[:part, :] = out_o[s * part : (s + 1) * part, :]
        for k in range(part // BLK):
            at = s * part + k * BLK
            stat = jnp.where(lane == 0, out_m[at : at + BLK, :], out_l[at : at + BLK, :])
            target[part + 8 * k : part + 8 * k + 8, :] = stat.T[:8]


def prefix_partials(queries, kv):
    part = queries[0].shape[0]
    one = jax.ShapeDtypeStruct((part + 8 * (part // BLK), HD), F32)
    whole = pltpu.VMEM((XS * part, HD), F32)
    return pl.pallas_call(
        prefix_kernel,
        out_shape=(one,) * XS,
        in_specs=[VMEM] * (XS + 1),
        out_specs=(VMEM,) * XS,
        scratch_shapes=[pltpu.VMEM((XS * part, HD), BF16), whole, whole, whole],
        compiler_params=params(),
        cost_estimate=cost(6),
        name="prefix_partials",
    )(*queries, kv)


def final_kernel(me, slot_req, flags, ret, lo, lm, ll, p0, p1, p2, p3, out, top, total, acc, turned, past):
    req, rows, _ = lo.shape
    n = ret.shape[0]
    batch = min(16, n)
    body = CAP * rows
    part = req * rows
    tiles = part // BLK
    per = BLK // rows
    parts = (p0, p1, p2, p3)
    past[...] = jnp.concatenate([p[part:, :] for p in parts], axis=0).T
    for g in range(n // batch):
        turned[g] = ret[g * batch : (g + 1) * batch, body : body + 8, :].reshape(batch * 8, BLK).T
    mine = pl.multiple_of(lax.rem(me[0], per) * rows, rows)

    def past_stat(p, r, field):
        col = (p * tiles + r // per) * 8 + field
        return past[(r % per) * rows : (r % per + 1) * rows, col : col + 1]

    for r in range(req):
        use = flags[r] == 1
        peak = lm[r]
        for p in range(XS):
            peak = jnp.maximum(peak, jnp.where(use, past_stat(p, r, 0), NEG))
        top[r] = peak
    for g in range(n // batch):
        stats = turned[g, pl.ds(mine, rows), :]
        for i in range(batch):
            for c in range(CAP):
                r = slot_req[(g * batch + i) * CAP + c]
                col = 8 * i + 2 * c
                top[r] = jnp.maximum(top[r], stats[:, col : col + 1])
    for r in range(req):
        use = flags[r] == 1
        peak = top[r]
        factor = jnp.exp(lm[r] - peak)
        sum_l, sum_o = ll[r] * factor, lo[r] * factor
        for p in range(XS):
            factor = jnp.exp(jnp.where(use, past_stat(p, r, 0), NEG) - peak)
            sum_l = sum_l + past_stat(p, r, 1) * factor
            sum_o = sum_o + parts[p][r * rows : (r + 1) * rows, :] * factor
        total[r] = sum_l
        acc[r] = sum_o
    for g in range(n // batch):
        stats = turned[g, pl.ds(mine, rows), :]
        for i in range(batch):
            for c in range(CAP):
                s = g * batch + i
                r = slot_req[s * CAP + c]
                col = 8 * i + 2 * c
                factor = jnp.exp(stats[:, col : col + 1] - top[r])
                total[r] += stats[:, col + 1 : col + 2] * factor
                acc[r] += ret[s, c * rows : (c + 1) * rows, :] * factor
    for r in range(req):
        out[r] = (acc[r] / total[r]).astype(BF16)


def final(me, slot_req, flags, ret, here, past):
    req, rows, _ = here[0].shape
    n = ret.shape[0]
    batch = min(16, n)
    whole = pltpu.VMEM((req, rows, HD), F32)
    return pl.pallas_call(
        final_kernel,
        out_shape=jax.ShapeDtypeStruct((req, rows, HD), BF16),
        in_specs=[SMEM, SMEM, SMEM] + [VMEM] * (4 + XS),
        out_specs=VMEM,
        scratch_shapes=[
            whole,
            whole,
            whole,
            pltpu.VMEM((n // batch, BLK, batch * 8), F32),
            pltpu.VMEM((BLK, XS * (req * rows // BLK) * 8), F32),
        ],
        compiler_params=params(),
        cost_estimate=cost(3),
        name="final",
    )(me, slot_req, flags, ret, *here, *past)


def after(value, *others):
    return lax.optimization_barrier((value, others))[0]


def per_device(queries, new_kv, pool, page, lengths, outbox, prefix_store, owner, flags):
    req, steps, width = queries.shape
    pool_size = pool.shape[0]
    rows = steps * (width // HD)
    n = lax.axis_size("inst")
    shares = lax.axis_size("tp")
    ys = n // (XS * ZS)
    plane = ys * ZS
    me = lax.axis_index("inst").astype(jnp.int32)
    owned = owner[0]

    def index(y, x, z):
        return ((y % ys) * XS + x % XS) * ZS + z % ZS

    def move(value, dy, dx, dz):
        pairs = [
            (index(y, x, z), index(y + dy, x + dx, z + dz))
            for y in range(ys)
            for x in range(XS)
            for z in range(ZS)
        ]
        return lax.ppermute(value, "inst", pairs)

    steps_out = ((0, 0, 0), (0, 0, 1), (0, 1, 0), (1, 0, 0))
    wide = prefix_store.shape[1] // len(steps_out)
    columns = []
    holders = []
    for k, (dy, dx, dz) in enumerate(steps_out):
        part = prefix_store[:, k * wide : (k + 1) * wide]
        columns.append(move(part, dy, dx, dz) if k else part)
        holders.append(index(owned // (XS * ZS) + dy, owned // ZS + dx, owned + dz))
    hold = sum(jnp.where(me == holders[k], k, 0) for k in range(1, len(steps_out)))
    spots = [
        ((i // ZS) % XS) * plane + (i // (XS * ZS)) * ZS + i % ZS for i in range(n)
    ]

    q = queries.reshape(req, rows, HD)
    local, slot_req, counts = prep(page, lengths, pool_size, n * CAP)
    pay = pack(spots, slot_req, counts, hold.reshape(1), q, columns)
    asked = lax.all_to_all(pay, "inst", split_axis=0, concat_axis=0, tiled=True)
    flat = after(q.reshape(req * rows, HD), pay)
    guests = [flat] + [move(flat, 0, s, 0) for s in range(1, XS)]
    fresh = jnp.pad(new_kv, ((0, 0), (0, 16 - steps), (0, 0)))
    here = local_partials(local, pool, q, fresh)
    head = CAP * rows + 16
    piece = jnp.concatenate(
        [
            lax.dynamic_slice(asked, (h, head, 0), (1, asked.shape[1] - head, HD))
            for h in holders
        ],
        axis=0,
    ).reshape(shares, -1, HD)
    piece = lax.all_to_all(
        after(piece, *guests, *here), "tp", split_axis=0, concat_axis=0, tiled=True
    )
    ret = remote_partials(outbox.reshape(-1), pool, asked, rows)
    planes = [[index(y, x, z) for y in range(ys) for z in range(ZS)] for x in range(XS)]
    prefix = lax.all_to_all(
        jnp.broadcast_to(after(piece, ret)[None], (plane,) + piece.shape),
        "inst",
        split_axis=0,
        concat_axis=0,
        tiled=True,
        axis_index_groups=planes,
    )
    back = lax.all_to_all(after(ret, prefix), "inst", split_axis=0, concat_axis=0, tiled=True)
    past = prefix_partials(guests, prefix)
    past = [past[0]] + [move(past[s], 0, -s, 0) for s in range(1, XS)]
    out = final(me.reshape(1), slot_req, flags, back, here, past)
    return out.reshape(req, steps, width)


def solution(mesh):
    placed = (
        P("inst", None, "tp"),
        P("inst", None, "tp"),
        P("inst", None, "tp"),
        P("inst", None),
        P("inst"),
        P("inst", None, None),
        P(("inst", "tp"), None),
        P(),
        P("inst"),
    )
    return jax.shard_map(
        per_device, mesh=mesh, in_specs=placed, out_specs=P("inst", None, "tp"), check_vma=False
    )
```

```python
import functools

import jax
import jax.numpy as jnp
from jax import lax
from jax.experimental import pallas as pl
from jax.experimental.pallas import tpu as pltpu
from jax.sharding import PartitionSpec as P

HD = 128
BLK = 128
CAP = 2
KEPT = 16
NEG = -1e30
XS = 4
ZS = 2
F32 = jnp.float32
BF16 = jnp.bfloat16

VMEM = pl.BlockSpec(memory_space=pltpu.VMEM)
SMEM = pl.BlockSpec(memory_space=pltpu.SMEM)


def params():
    return pltpu.CompilerParams(vmem_limit_bytes=16 * 1024 * 1024)


def cost(us):
    return pl.CostEstimate(flops=0, bytes_accessed=int(us * 3.0e6), transcendentals=0)


def dot_nt(a, b):
    return lax.dot_general(a, b, (((1,), (1,)), ((), ())), preferred_element_type=F32)


def dot_nn(a, b):
    return lax.dot_general(a, b, (((1,), (0,)), ((), ())), preferred_element_type=F32)


def with_ones(values):
    return jnp.concatenate([values, jnp.ones_like(values)], axis=1)


def batch_partials(jobs):
    rows = jobs[0][0].shape[0]
    scores = jnp.concatenate([dot_nt(q, keys) for q, keys, _, _ in jobs], axis=0) * (HD ** -0.5)
    masked = jobs[0][3] is not None
    if masked:
        valid = jnp.concatenate([job[3] for job in jobs], axis=0)
        scores = jnp.where(valid, scores, NEG)
    top = jnp.max(scores, axis=-1, keepdims=True)
    weights = jnp.exp(scores - top)
    if masked:
        weights = jnp.where(valid, weights, 0.0)
    weights = weights.astype(BF16)
    found = []
    for i, (_, _, values, _) in enumerate(jobs):
        both = dot_nn(weights[i * rows : (i + 1) * rows], with_ones(values))
        found.append((top[i * rows : (i + 1) * rows], both[:, HD:], both[:, :HD]))
    return found


def prep_kernel(pool_size, page, lens, local, slot_req, counts):
    for k in range(KEPT):
        for field in range(3):
            local[field, k] = 0

    def request(r, kept):
        length = lens[r]

        def block(j, kept):
            b = page[r, j]
            valid = jnp.minimum(length - j * BLK, BLK)
            away = b >= pool_size

            @pl.when(away)
            def _():
                slot_req[b - pool_size] = r
                counts[b - pool_size] = valid

            @pl.when(jnp.logical_not(away))
            def _():
                local[0, kept] = b
                local[1, kept] = r
                local[2, kept] = valid

            return kept + jnp.where(away, 0, 1)

        return lax.fori_loop(0, lax.shift_right_logical(length + BLK - 1, 7), block, kept)

    lax.fori_loop(0, lens.shape[0], request, 0)


def prep(page, lengths, pool_size, slots):
    return pl.pallas_call(
        functools.partial(prep_kernel, pool_size),
        out_shape=(
            jax.ShapeDtypeStruct((3, KEPT), jnp.int32),
            jax.ShapeDtypeStruct((slots,), jnp.int32),
            jax.ShapeDtypeStruct((slots,), jnp.int32),
        ),
        in_specs=[SMEM, SMEM],
        out_specs=(SMEM, SMEM, SMEM),
        compiler_params=params(),
        cost_estimate=cost(3),
        name="prep",
    )(page, lengths)


def pack_kernel(spots, slot_req, counts, hold, q, *refs):
    sources, pay = refs[:-1], refs[-1]
    rows = q.shape[1]
    body = CAP * rows
    upper = lax.broadcasted_iota(jnp.int32, (16, HD), 0) < 8
    tokens = sources[0].shape[0] // len(spots)
    most = sources[0].shape[1] // HD
    for d in range(len(spots)):
        for c in range(CAP):
            pay[d, c * rows : (c + 1) * rows, :] = q[slot_req[CAP * d + c]]
        tile = jnp.where(upper, counts[CAP * d], counts[CAP * d + 1])
        pay[d, body : body + 16, :] = tile.astype(F32).astype(BF16)
    for k, source in enumerate(sources):

        @pl.when(hold[0] == k)
        def _():
            for d, spot in enumerate(spots):
                for j in range(most):
                    at = body + 16 + j * tokens
                    col = (j % (source.shape[1] // HD)) * HD
                    pay[d, at : at + tokens, :] = source[
                        spot * tokens : (spot + 1) * tokens, col : col + HD
                    ]


def pack(spots, slot_req, counts, hold, q, columns):
    n = len(spots)
    rows = q.shape[1]
    held, wide = columns[0].shape
    height = CAP * rows + 16 + (wide // HD) * (held // n)
    return pl.pallas_call(
        functools.partial(pack_kernel, spots),
        out_shape=jax.ShapeDtypeStruct((n, height, HD), BF16),
        in_specs=[SMEM, SMEM, SMEM, VMEM] + [VMEM] * len(columns),
        out_specs=VMEM,
        compiler_params=params(),
        cost_estimate=cost(1.5),
        name="pack",
    )(slot_req, counts, hold, q, *columns)


def gather_kernel(spans, holders, asked, out):
    first = 0
    head = asked.shape[1] - spans[0]
    flat = out.shape[1]
    for k, span in enumerate(spans):
        for h in range(span // flat):
            at = head + h * flat
            out[first] = asked[holders[k], at : at + flat, :]
            first += 1


def gather(spans, holders, asked, shares):
    return pl.pallas_call(
        functools.partial(gather_kernel, spans),
        out_shape=jax.ShapeDtypeStruct((shares, sum(spans) // shares, HD), BF16),
        in_specs=[SMEM, VMEM],
        out_specs=VMEM,
        compiler_params=params(),
        cost_estimate=cost(0.5),
        name="gather",
    )(holders, asked)


def remote_kernel(outbox, pool, pay, ret):
    n = pay.shape[0]
    rows = (ret.shape[1] - 8) // CAP
    each = BLK // rows
    lane = lax.broadcasted_iota(jnp.int32, (rows, BLK), 1)

    def group(g, carry):
        jobs = []
        for i in range(each):
            d = g * each + i
            marks = pay[d, CAP * rows : CAP * rows + 16, :].astype(F32).astype(jnp.int32)
            for c in range(CAP):
                kv = pool[outbox[d * CAP + c]]
                valid = lane < marks[8 * c : 8 * c + 1, :]
                jobs.append((pay[d, c * rows : (c + 1) * rows, :], kv[:, :HD], kv[:, HD:], valid))
        found = batch_partials(jobs)
        stats = []
        for i in range(each):
            stat = jnp.zeros((rows, BLK), F32)
            for c in range(CAP):
                top, total, out = found[i * CAP + c]
                ret[g * each + i, c * rows : (c + 1) * rows, :] = out
                stat = jnp.where(lane == 2 * c, top, stat)
                stat = jnp.where(lane == 2 * c + 1, total, stat)
            stats.append(stat)
        turned = jnp.concatenate(stats, axis=0).T[:8]
        for i in range(each):
            ret[g * each + i, CAP * rows : CAP * rows + 8, :] = turned
        return carry

    lax.fori_loop(0, n // each, group, 0)


def remote_partials(outbox, pool, pay, rows):
    n = pay.shape[0]
    return pl.pallas_call(
        remote_kernel,
        out_shape=jax.ShapeDtypeStruct((n, CAP * rows + 8, HD), F32),
        in_specs=[SMEM, VMEM, VMEM],
        out_specs=VMEM,
        compiler_params=params(),
        cost_estimate=cost(6),
        name="remote_partials",
    )(outbox, pool, pay)


def local_kernel(local, pool, q, fresh, out_o, out_m, out_l):
    req, rows, _ = q.shape
    steps = rows // 8
    keys = fresh.shape[1]
    step = lax.broadcasted_iota(jnp.int32, (rows, keys), 0) // 8
    place = lax.broadcasted_iota(jnp.int32, (rows, keys), 1)
    causal = (place <= step) & (place < steps)
    found = batch_partials([(q[r], fresh[r, :, :HD], fresh[r, :, HD:], causal) for r in range(req)])
    for r, (top, total, out) in enumerate(found):
        out_o[r] = out
        out_l[r] = total
        out_m[r] = jnp.broadcast_to(top, (rows, HD))
    lane = lax.broadcasted_iota(jnp.int32, (rows, BLK), 1)

    def batch(g, carry):
        jobs = []
        for i in range(8):
            k = g * 8 + i
            kv = pool[local[0, k]]
            jobs.append((q[local[1, k]], kv[:, :HD], kv[:, HD:], lane < local[2, k]))
        found = batch_partials(jobs)
        for i in range(8):
            r = local[1, g * 8 + i]
            top, total, out = found[i]
            old = out_m[r]
            new = jnp.maximum(old, top)
            keep, add = jnp.exp(old - new), jnp.exp(top - new)
            out_m[r] = new
            out_l[r] = out_l[r] * keep + total * add
            out_o[r] = out_o[r] * keep + out * add
        return carry

    lax.fori_loop(0, KEPT // 8, batch, 0)


def local_partials(local, pool, q, fresh):
    one = jax.ShapeDtypeStruct(q.shape, F32)
    return pl.pallas_call(
        local_kernel,
        out_shape=(one, one, one),
        in_specs=[SMEM, VMEM, VMEM, VMEM],
        out_specs=(VMEM, VMEM, VMEM),
        compiler_params=params(),
        cost_estimate=cost(6),
        name="local_partials",
    )(local, pool, q, fresh)


def prefix_kernel(q0, q1, q2, q3, kv, p0, p1, p2, p3, q, out_o, out_m, out_l):
    chips, cores, double = kv.shape[1], kv.shape[3], kv.shape[4]
    tokens = double // 2
    part = q0.shape[0]
    for s, source in enumerate((q0, q1, q2, q3)):
        q[s * part : (s + 1) * part, :] = source[...]
    out_o[...] = jnp.zeros_like(out_o)
    out_l[...] = jnp.zeros_like(out_l)
    out_m[...] = jnp.full_like(out_m, NEG)

    def pair(t, carry):
        jobs = []
        for b in range(cores):
            keys = kv[:, t, :, b, :tokens].reshape(BLK, HD)
            values = kv[:, t, :, b, tokens:].reshape(BLK, HD)
            jobs.append((q[...], keys, values, None))
        found = batch_partials(jobs)
        old = out_m[...]
        new = jnp.maximum(jnp.maximum(old, found[0][0]), found[1][0])
        keep = jnp.exp(old - new)
        acc_l, acc_o = out_l[...] * keep, out_o[...] * keep
        for top, total, out in found:
            add = jnp.exp(top - new)
            acc_l = acc_l + total * add
            acc_o = acc_o + out * add
        out_m[...] = new
        out_l[...] = acc_l
        out_o[...] = acc_o
        return carry

    lax.fori_loop(0, chips, pair, 0)
    lane = lax.broadcasted_iota(jnp.int32, (BLK, HD), 1)
    for s, target in enumerate((p0, p1, p2, p3)):
        target[:part, :] = out_o[s * part : (s + 1) * part, :]
        for k in range(part // BLK):
            at = s * part + k * BLK
            stat = jnp.where(lane == 0, out_m[at : at + BLK, :], out_l[at : at + BLK, :])
            target[part + 8 * k : part + 8 * k + 8, :] = stat.T[:8]


def prefix_partials(queries, kv):
    part = queries[0].shape[0]
    one = jax.ShapeDtypeStruct((part + 8 * (part // BLK), HD), F32)
    whole = pltpu.VMEM((XS * part, HD), F32)
    return pl.pallas_call(
        prefix_kernel,
        out_shape=(one,) * XS,
        in_specs=[VMEM] * (XS + 1),
        out_specs=(VMEM,) * XS,
        scratch_shapes=[pltpu.VMEM((XS * part, HD), BF16), whole, whole, whole],
        compiler_params=params(),
        cost_estimate=cost(6),
        name="prefix_partials",
    )(*queries, kv)


def merge_kernel(me, slot_req, ret, lo, lm, ll, acc, top, total, turned):
    req, rows, _ = lo.shape
    n = ret.shape[0]
    batch = min(16, n)
    body = CAP * rows
    per = BLK // rows
    for g in range(n // batch):
        turned[g] = ret[g * batch : (g + 1) * batch, body : body + 8, :].reshape(batch * 8, BLK).T
    mine = pl.multiple_of(lax.rem(me[0], per) * rows, rows)
    top[...] = lm[...]
    for g in range(n // batch):
        stats = turned[g, pl.ds(mine, rows), :]
        for i in range(batch):
            for c in range(CAP):
                r = slot_req[(g * batch + i) * CAP + c]
                col = 8 * i + 2 * c
                top[r] = jnp.maximum(top[r], stats[:, col : col + 1])
    for r in range(req):
        factor = jnp.exp(lm[r] - top[r])
        total[r] = ll[r] * factor
        acc[r] = lo[r] * factor
    for g in range(n // batch):
        stats = turned[g, pl.ds(mine, rows), :]
        for i in range(batch):
            for c in range(CAP):
                s = g * batch + i
                r = slot_req[s * CAP + c]
                col = 8 * i + 2 * c
                factor = jnp.exp(stats[:, col : col + 1] - top[r])
                total[r] += stats[:, col + 1 : col + 2] * factor
                acc[r] += ret[s, c * rows : (c + 1) * rows, :] * factor


def merge(me, slot_req, ret, here):
    n = ret.shape[0]
    batch = min(16, n)
    one = jax.ShapeDtypeStruct(here[0].shape, F32)
    return pl.pallas_call(
        merge_kernel,
        out_shape=(one, one, one),
        in_specs=[SMEM, SMEM] + [VMEM] * 4,
        out_specs=(VMEM, VMEM, VMEM),
        scratch_shapes=[pltpu.VMEM((n // batch, BLK, batch * 8), F32)],
        compiler_params=params(),
        cost_estimate=cost(2),
        name="merge",
    )(me, slot_req, ret, *here)


def final_kernel(flags, acc, top, total, p0, p1, p2, p3, out, past):
    req, rows, _ = acc.shape
    part = req * rows
    tiles = part // BLK
    per = BLK // rows
    parts = (p0, p1, p2, p3)
    past[...] = jnp.concatenate([p[part:, :] for p in parts], axis=0).T
    for r in range(req):
        use = flags[r] == 1
        at = (r % per) * rows
        tops, sums = [], []
        for p in range(XS):
            col = (p * tiles + r // per) * 8
            stat = past[at : at + rows, col : col + 2]
            tops.append(jnp.where(use, stat[:, 0:1], NEG))
            sums.append(stat[:, 1:2])
        peak = top[r]
        for found in tops:
            peak = jnp.maximum(peak, found)
        factor = jnp.exp(top[r] - peak)
        sum_l, sum_o = total[r] * factor, acc[r] * factor
        for p in range(XS):
            factor = jnp.exp(tops[p] - peak)
            sum_l = sum_l + sums[p] * factor
            sum_o = sum_o + parts[p][r * rows : (r + 1) * rows, :] * factor
        out[r] = (sum_o / sum_l).astype(BF16)


def final(flags, merged, past):
    req, rows, _ = merged[0].shape
    return pl.pallas_call(
        final_kernel,
        out_shape=jax.ShapeDtypeStruct((req, rows, HD), BF16),
        in_specs=[SMEM] + [VMEM] * (3 + XS),
        out_specs=VMEM,
        scratch_shapes=[pltpu.VMEM((BLK, XS * (req * rows // BLK) * 8), F32)],
        compiler_params=params(),
        cost_estimate=cost(1),
        name="final",
    )(flags, *merged, *past)


def after(value, *others):
    return lax.optimization_barrier((value, others))[0]


def per_device(queries, new_kv, pool, page, lengths, outbox, prefix_store, owner, flags):
    req, steps, width = queries.shape
    pool_size = pool.shape[0]
    rows = steps * (width // HD)
    n = lax.axis_size("inst")
    shares = lax.axis_size("tp")
    ys = n // (XS * ZS)
    plane = ys * ZS
    me = lax.axis_index("inst").astype(jnp.int32)
    owned = owner[0]

    def index(y, x, z):
        return ((y % ys) * XS + x % XS) * ZS + z % ZS

    def move(value, dy, dx, dz):
        pairs = [
            (index(y, x, z), index(y + dy, x + dx, z + dz))
            for y in range(ys)
            for x in range(XS)
            for z in range(ZS)
        ]
        return lax.ppermute(value, "inst", pairs)

    steps_out = (
        (2, 0, 0, 0),
        (2, 0, 0, 1),
        (1, 0, 1, 0),
        (1, 0, -1, 0),
        (1, 1, 0, 0),
        (1, -1, 0, 0),
    )
    head_width = prefix_store.shape[1] // shares
    columns = []
    holders = []
    first = 0
    for heads, dy, dx, dz in steps_out:
        part = prefix_store[:, first * head_width : (first + heads) * head_width]
        first += heads
        columns.append(move(part, dy, dx, dz) if holders else part)
        holders.append(index(owned // (XS * ZS) + dy, owned // ZS + dx, owned + dz))
    hold = sum(jnp.where(me == holders[k], k, 0) for k in range(1, len(steps_out)))
    spots = [
        ((i // ZS) % XS) * plane + (i // (XS * ZS)) * ZS + i % ZS for i in range(n)
    ]

    q = queries.reshape(req, rows, HD)
    local, slot_req, counts = prep(page, lengths, pool_size, n * CAP)
    tokens = prefix_store.shape[0] // n
    spans = tuple(heads * 2 * tokens for heads, _, _, _ in steps_out)
    pay = pack(spots, slot_req, counts, hold.reshape(1), q, columns)
    asked = lax.all_to_all(pay, "inst", split_axis=0, concat_axis=0, tiled=True)
    fresh = jnp.pad(new_kv, ((0, 0), (0, 16 - steps), (0, 0)))
    here = local_partials(local, pool, q, fresh)
    piece = gather(spans, jnp.stack(holders).astype(jnp.int32), asked, shares)
    piece = after(piece, *here)

    tp = lax.axis_index("tp").astype(jnp.int32)
    cores = 2
    chips = shares // cores
    core = tp % cores
    piece = piece.reshape(chips, cores, -1, HD)
    mine = lax.dynamic_index_in_dim(piece, core, 1, keepdims=False)
    other = lax.dynamic_index_in_dim(piece, 1 - core, 1, keepdims=False)
    other = lax.ppermute(other, "tp", [(t, t ^ 1) for t in range(shares)])
    both = jnp.stack([mine, other], axis=1)
    sheets = [
        [
            index(y, x, z) * shares + chip * cores + c
            for y in range(ys)
            for chip in range(chips)
            for z in range(ZS)
        ]
        for x in range(XS)
        for c in range(cores)
    ]
    flat = after(q.reshape(req * rows, HD), both)
    guests = [flat] + [move(flat, 0, s, 0) for s in range(1, XS)]
    whole = (ys, chips, ZS) + both.shape[1:]
    spread = jnp.broadcast_to(both[None, :, None], whole)
    prefix = lax.all_to_all(
        spread.reshape((-1,) + both.shape[1:]),
        ("inst", "tp"),
        split_axis=0,
        concat_axis=0,
        tiled=True,
        axis_index_groups=sheets,
    ).reshape(whole)
    ret = remote_partials(outbox.reshape(-1), pool, asked, rows)
    back = lax.all_to_all(after(ret, prefix, *guests), "inst", split_axis=0, concat_axis=0, tiled=True)
    past = prefix_partials(guests, prefix)
    past = [past[0]] + [move(past[s], 0, -s, 0) for s in range(1, XS)]
    merged = merge(me.reshape(1), slot_req, back, here)
    out = final(flags, merged, past)
    return out.reshape(req, steps, width)


def solution(mesh):
    placed = (
        P("inst", None, "tp"),
        P("inst", None, "tp"),
        P("inst", None, "tp"),
        P("inst", None),
        P("inst"),
        P("inst", None, None),
        P(("inst", "tp"), None),
        P(),
        P("inst"),
    )
    return jax.shard_map(
        per_device, mesh=mesh, in_specs=placed, out_specs=P("inst", None, "tp"), check_vma=False
    )
```

```python
import functools

import jax
import jax.numpy as jnp
from jax import lax
from jax.experimental import pallas as pl
from jax.experimental.pallas import tpu as pltpu
from jax.sharding import PartitionSpec as P

HD = 128
BLK = 128
CAP = 2
KEPT = 16
NEG = -1e30
XS = 4
ZS = 2
F32 = jnp.float32
BF16 = jnp.bfloat16

VMEM = pl.BlockSpec(memory_space=pltpu.VMEM)
SMEM = pl.BlockSpec(memory_space=pltpu.SMEM)


def params():
    return pltpu.CompilerParams(vmem_limit_bytes=16 * 1024 * 1024)


def cost(us):
    return pl.CostEstimate(flops=0, bytes_accessed=int(us * 3.0e6), transcendentals=0)


def dot_nt(a, b):
    return lax.dot_general(a, b, (((1,), (1,)), ((), ())), preferred_element_type=F32)


def dot_nn(a, b):
    return lax.dot_general(a, b, (((1,), (0,)), ((), ())), preferred_element_type=F32)


def with_ones(values):
    return jnp.concatenate([values, jnp.ones_like(values)], axis=1)


def batch_partials(jobs):
    rows = jobs[0][0].shape[0]
    scores = jnp.concatenate([dot_nt(q, keys) for q, keys, _, _ in jobs], axis=0) * (HD ** -0.5)
    masked = jobs[0][3] is not None
    if masked:
        valid = jnp.concatenate([job[3] for job in jobs], axis=0)
        scores = jnp.where(valid, scores, NEG)
    top = jnp.max(scores, axis=-1, keepdims=True)
    weights = jnp.exp(scores - top)
    if masked:
        weights = jnp.where(valid, weights, 0.0)
    weights = weights.astype(BF16)
    found = []
    for i, (_, _, values, _) in enumerate(jobs):
        both = dot_nn(weights[i * rows : (i + 1) * rows], with_ones(values))
        found.append((top[i * rows : (i + 1) * rows], both[:, HD:], both[:, :HD]))
    return found


def prep_kernel(pool_size, page, lens, local, slot_req, counts):
    for k in range(KEPT):
        for field in range(3):
            local[field, k] = 0

    def request(r, kept):
        length = lens[r]

        def block(j, kept):
            b = page[r, j]
            valid = jnp.minimum(length - j * BLK, BLK)
            away = b >= pool_size

            @pl.when(away)
            def _():
                slot_req[b - pool_size] = r
                counts[b - pool_size] = valid

            @pl.when(jnp.logical_not(away))
            def _():
                local[0, kept] = b
                local[1, kept] = r
                local[2, kept] = valid

            return kept + jnp.where(away, 0, 1)

        return lax.fori_loop(0, lax.shift_right_logical(length + BLK - 1, 7), block, kept)

    lax.fori_loop(0, lens.shape[0], request, 0)


def prep(page, lengths, pool_size, slots):
    return pl.pallas_call(
        functools.partial(prep_kernel, pool_size),
        out_shape=(
            jax.ShapeDtypeStruct((3, KEPT), jnp.int32),
            jax.ShapeDtypeStruct((slots,), jnp.int32),
            jax.ShapeDtypeStruct((slots,), jnp.int32),
        ),
        in_specs=[SMEM, SMEM],
        out_specs=(SMEM, SMEM, SMEM),
        compiler_params=params(),
        cost_estimate=cost(3),
        name="prep",
    )(page, lengths)


def pack_kernel(spots, slot_req, counts, hold, q, *refs):
    sources, pay = refs[:-1], refs[-1]
    rows = q.shape[1]
    body = CAP * rows
    upper = lax.broadcasted_iota(jnp.int32, (16, HD), 0) < 8
    tokens = sources[0].shape[0] // len(spots)
    most = sources[0].shape[1] // HD
    for d in range(len(spots)):
        for c in range(CAP):
            pay[d, c * rows : (c + 1) * rows, :] = q[slot_req[CAP * d + c]]
        tile = jnp.where(upper, counts[CAP * d], counts[CAP * d + 1])
        pay[d, body : body + 16, :] = tile.astype(F32).astype(BF16)
    for k, source in enumerate(sources):

        @pl.when(hold[0] == k)
        def _():
            for d, spot in enumerate(spots):
                for j in range(most):
                    at = body + 16 + j * tokens
                    col = (j % (source.shape[1] // HD)) * HD
                    pay[d, at : at + tokens, :] = source[
                        spot * tokens : (spot + 1) * tokens, col : col + HD
                    ]


def pack(spots, slot_req, counts, hold, q, columns):
    n = len(spots)
    rows = q.shape[1]
    held, wide = columns[0].shape
    height = CAP * rows + 16 + (wide // HD) * (held // n)
    return pl.pallas_call(
        functools.partial(pack_kernel, spots),
        out_shape=jax.ShapeDtypeStruct((n, height, HD), BF16),
        in_specs=[SMEM, SMEM, SMEM, VMEM] + [VMEM] * len(columns),
        out_specs=VMEM,
        compiler_params=params(),
        cost_estimate=cost(1.5),
        name="pack",
    )(slot_req, counts, hold, q, *columns)


def gather_kernel(units, holders, asked, out):
    tokens = out.shape[1] // 2
    head = asked.shape[1] - units[0] * tokens
    first = 0
    for k, count in enumerate(units):
        for j in range(count):
            half = (first % 2) * tokens
            at = head + j * tokens
            out[first // 2, half : half + tokens, :] = asked[holders[k], at : at + tokens, :]
            first += 1


def gather(units, holders, asked, tokens):
    return pl.pallas_call(
        functools.partial(gather_kernel, units),
        out_shape=jax.ShapeDtypeStruct((sum(units) // 2, 2 * tokens, HD), BF16),
        in_specs=[SMEM, VMEM],
        out_specs=VMEM,
        compiler_params=params(),
        cost_estimate=cost(0.5),
        name="gather",
    )(holders, asked)


def remote_kernel(outbox, pool, pay, ret):
    n = pay.shape[0]
    rows = (ret.shape[1] - 8) // CAP
    each = BLK // rows
    lane = lax.broadcasted_iota(jnp.int32, (rows, BLK), 1)

    def group(g, carry):
        jobs = []
        for i in range(each):
            d = g * each + i
            marks = pay[d, CAP * rows : CAP * rows + 16, :].astype(F32).astype(jnp.int32)
            for c in range(CAP):
                kv = pool[outbox[d * CAP + c]]
                valid = lane < marks[8 * c : 8 * c + 1, :]
                jobs.append((pay[d, c * rows : (c + 1) * rows, :], kv[:, :HD], kv[:, HD:], valid))
        found = batch_partials(jobs)
        stats = []
        for i in range(each):
            stat = jnp.zeros((rows, BLK), F32)
            for c in range(CAP):
                top, total, out = found[i * CAP + c]
                ret[g * each + i, c * rows : (c + 1) * rows, :] = out
                stat = jnp.where(lane == 2 * c, top, stat)
                stat = jnp.where(lane == 2 * c + 1, total, stat)
            stats.append(stat)
        turned = jnp.concatenate(stats, axis=0).T[:8]
        for i in range(each):
            ret[g * each + i, CAP * rows : CAP * rows + 8, :] = turned
        return carry

    lax.fori_loop(0, n // each, group, 0)


def remote_partials(outbox, pool, pay, rows):
    n = pay.shape[0]
    return pl.pallas_call(
        remote_kernel,
        out_shape=jax.ShapeDtypeStruct((n, CAP * rows + 8, HD), F32),
        in_specs=[SMEM, VMEM, VMEM],
        out_specs=VMEM,
        compiler_params=params(),
        cost_estimate=cost(6),
        name="remote_partials",
    )(outbox, pool, pay)


def local_kernel(local, pool, q, fresh, out_o, out_m, out_l):
    req, rows, _ = q.shape
    steps = rows // 8
    keys = fresh.shape[1]
    step = lax.broadcasted_iota(jnp.int32, (rows, keys), 0) // 8
    place = lax.broadcasted_iota(jnp.int32, (rows, keys), 1)
    causal = (place <= step) & (place < steps)
    found = batch_partials([(q[r], fresh[r, :, :HD], fresh[r, :, HD:], causal) for r in range(req)])
    for r, (top, total, out) in enumerate(found):
        out_o[r] = out
        out_l[r] = total
        out_m[r] = jnp.broadcast_to(top, (rows, HD))
    lane = lax.broadcasted_iota(jnp.int32, (rows, BLK), 1)

    def batch(g, carry):
        jobs = []
        for i in range(8):
            k = g * 8 + i
            kv = pool[local[0, k]]
            jobs.append((q[local[1, k]], kv[:, :HD], kv[:, HD:], lane < local[2, k]))
        found = batch_partials(jobs)
        for i in range(8):
            r = local[1, g * 8 + i]
            top, total, out = found[i]
            old = out_m[r]
            new = jnp.maximum(old, top)
            keep, add = jnp.exp(old - new), jnp.exp(top - new)
            out_m[r] = new
            out_l[r] = out_l[r] * keep + total * add
            out_o[r] = out_o[r] * keep + out * add
        return carry

    lax.fori_loop(0, KEPT // 8, batch, 0)


def local_partials(local, pool, q, fresh):
    one = jax.ShapeDtypeStruct(q.shape, F32)
    return pl.pallas_call(
        local_kernel,
        out_shape=(one, one, one),
        in_specs=[SMEM, VMEM, VMEM, VMEM],
        out_specs=(VMEM, VMEM, VMEM),
        compiler_params=params(),
        cost_estimate=cost(6),
        name="local_partials",
    )(local, pool, q, fresh)


def prefix_kernel(q0, q1, q2, q3, kv, p0, p1, p2, p3, q, out_o, out_m, out_l):
    chips, cores, double = kv.shape[1], kv.shape[3], kv.shape[4]
    tokens = double // 2
    part = q0.shape[0]
    for s, source in enumerate((q0, q1, q2, q3)):
        q[s * part : (s + 1) * part, :] = source[...]
    out_o[...] = jnp.zeros_like(out_o)
    out_l[...] = jnp.zeros_like(out_l)
    out_m[...] = jnp.full_like(out_m, NEG)

    def pair(t, carry):
        jobs = []
        for b in range(cores):
            keys = kv[:, t, :, b, :tokens].reshape(BLK, HD)
            values = kv[:, t, :, b, tokens:].reshape(BLK, HD)
            jobs.append((q[...], keys, values, None))
        found = batch_partials(jobs)
        old = out_m[...]
        new = jnp.maximum(jnp.maximum(old, found[0][0]), found[1][0])
        keep = jnp.exp(old - new)
        acc_l, acc_o = out_l[...] * keep, out_o[...] * keep
        for top, total, out in found:
            add = jnp.exp(top - new)
            acc_l = acc_l + total * add
            acc_o = acc_o + out * add
        out_m[...] = new
        out_l[...] = acc_l
        out_o[...] = acc_o
        return carry

    lax.fori_loop(0, chips, pair, 0)
    lane = lax.broadcasted_iota(jnp.int32, (BLK, HD), 1)
    for s, target in enumerate((p0, p1, p2, p3)):
        target[:part, :] = out_o[s * part : (s + 1) * part, :]
        for k in range(part // BLK):
            at = s * part + k * BLK
            stat = jnp.where(lane == 0, out_m[at : at + BLK, :], out_l[at : at + BLK, :])
            target[part + 8 * k : part + 8 * k + 8, :] = stat.T[:8]


def prefix_partials(queries, kv):
    part = queries[0].shape[0]
    one = jax.ShapeDtypeStruct((part + 8 * (part // BLK), HD), F32)
    whole = pltpu.VMEM((XS * part, HD), F32)
    return pl.pallas_call(
        prefix_kernel,
        out_shape=(one,) * XS,
        in_specs=[VMEM] * (XS + 1),
        out_specs=(VMEM,) * XS,
        scratch_shapes=[pltpu.VMEM((XS * part, HD), BF16), whole, whole, whole],
        compiler_params=params(),
        cost_estimate=cost(6),
        name="prefix_partials",
    )(*queries, kv)


def merge_kernel(me, slot_req, ret, lo, lm, ll, acc, top, total, turned):
    req, rows, _ = lo.shape
    n = ret.shape[0]
    batch = min(16, n)
    body = CAP * rows
    per = BLK // rows
    for g in range(n // batch):
        turned[g] = ret[g * batch : (g + 1) * batch, body : body + 8, :].reshape(batch * 8, BLK).T
    mine = pl.multiple_of(lax.rem(me[0], per) * rows, rows)
    top[...] = lm[...]
    for g in range(n // batch):
        stats = turned[g, pl.ds(mine, rows), :]
        for i in range(batch):
            for c in range(CAP):
                r = slot_req[(g * batch + i) * CAP + c]
                col = 8 * i + 2 * c
                top[r] = jnp.maximum(top[r], stats[:, col : col + 1])
    for r in range(req):
        factor = jnp.exp(lm[r] - top[r])
        total[r] = ll[r] * factor
        acc[r] = lo[r] * factor
    for g in range(n // batch):
        stats = turned[g, pl.ds(mine, rows), :]
        for i in range(batch):
            for c in range(CAP):
                s = g * batch + i
                r = slot_req[s * CAP + c]
                col = 8 * i + 2 * c
                factor = jnp.exp(stats[:, col : col + 1] - top[r])
                total[r] += stats[:, col + 1 : col + 2] * factor
                acc[r] += ret[s, c * rows : (c + 1) * rows, :] * factor


def merge(me, slot_req, ret, here):
    n = ret.shape[0]
    batch = min(16, n)
    one = jax.ShapeDtypeStruct(here[0].shape, F32)
    return pl.pallas_call(
        merge_kernel,
        out_shape=(one, one, one),
        in_specs=[SMEM, SMEM] + [VMEM] * 4,
        out_specs=(VMEM, VMEM, VMEM),
        scratch_shapes=[pltpu.VMEM((n // batch, BLK, batch * 8), F32)],
        compiler_params=params(),
        cost_estimate=cost(2),
        name="merge",
    )(me, slot_req, ret, *here)


def final_kernel(flags, acc, top, total, p0, p1, p2, p3, out, past):
    req, rows, _ = acc.shape
    part = req * rows
    tiles = part // BLK
    per = BLK // rows
    parts = (p0, p1, p2, p3)
    past[...] = jnp.concatenate([p[part:, :] for p in parts], axis=0).T
    for r in range(req):
        use = flags[r] == 1
        at = (r % per) * rows
        tops, sums = [], []
        for p in range(XS):
            col = (p * tiles + r // per) * 8
            stat = past[at : at + rows, col : col + 2]
            tops.append(jnp.where(use, stat[:, 0:1], NEG))
            sums.append(stat[:, 1:2])
        peak = top[r]
        for found in tops:
            peak = jnp.maximum(peak, found)
        factor = jnp.exp(top[r] - peak)
        sum_l, sum_o = total[r] * factor, acc[r] * factor
        for p in range(XS):
            factor = jnp.exp(tops[p] - peak)
            sum_l = sum_l + sums[p] * factor
            sum_o = sum_o + parts[p][r * rows : (r + 1) * rows, :] * factor
        out[r] = (sum_o / sum_l).astype(BF16)


def final(flags, merged, past):
    req, rows, _ = merged[0].shape
    return pl.pallas_call(
        final_kernel,
        out_shape=jax.ShapeDtypeStruct((req, rows, HD), BF16),
        in_specs=[SMEM] + [VMEM] * (3 + XS),
        out_specs=VMEM,
        scratch_shapes=[pltpu.VMEM((BLK, XS * (req * rows // BLK) * 8), F32)],
        compiler_params=params(),
        cost_estimate=cost(1),
        name="final",
    )(flags, *merged, *past)


def after(value, *others):
    return lax.optimization_barrier((value, others))[0]


def per_device(queries, new_kv, pool, page, lengths, outbox, prefix_store, owner, flags):
    req, steps, width = queries.shape
    pool_size = pool.shape[0]
    rows = steps * (width // HD)
    n = lax.axis_size("inst")
    shares = lax.axis_size("tp")
    ys = n // (XS * ZS)
    plane = ys * ZS
    me = lax.axis_index("inst").astype(jnp.int32)
    owned = owner[0]

    def index(y, x, z):
        return ((y % ys) * XS + x % XS) * ZS + z % ZS

    def move(value, dy, dx, dz):
        pairs = [
            (index(y, x, z), index(y + dy, x + dx, z + dz))
            for y in range(ys)
            for x in range(XS)
            for z in range(ZS)
        ]
        return lax.ppermute(value, "inst", pairs)

    steps_out = (
        (3, 0, 0, 0),
        (3, 0, 0, 1),
        (3, 0, 1, 0),
        (3, 0, -1, 0),
        (2, 1, 0, 0),
        (2, -1, 0, 0),
    )
    columns = []
    holders = []
    first = 0
    for units, dy, dx, dz in steps_out:
        part = prefix_store[:, first * HD : (first + units) * HD]
        first += units
        columns.append(move(part, dy, dx, dz) if holders else part)
        holders.append(index(owned // (XS * ZS) + dy, owned // ZS + dx, owned + dz))
    hold = sum(jnp.where(me == holders[k], k, 0) for k in range(1, len(steps_out)))
    spots = [
        ((i // ZS) % XS) * plane + (i // (XS * ZS)) * ZS + i % ZS for i in range(n)
    ]

    q = queries.reshape(req, rows, HD)
    local, slot_req, counts = prep(page, lengths, pool_size, n * CAP)
    tokens = prefix_store.shape[0] // n
    tokens = prefix_store.shape[0] // n
    units = tuple(step[0] for step in steps_out)
    pay = pack(spots, slot_req, counts, hold.reshape(1), q, columns)
    asked = lax.all_to_all(pay, "inst", split_axis=0, concat_axis=0, tiled=True)
    fresh = jnp.pad(new_kv, ((0, 0), (0, 16 - steps), (0, 0)))
    here = local_partials(local, pool, q, fresh)
    piece = gather(units, jnp.stack(holders).astype(jnp.int32), asked, tokens)
    piece = after(piece, *here)

    tp = lax.axis_index("tp").astype(jnp.int32)
    cores = 2
    chips = shares // cores
    core = tp % cores
    piece = piece.reshape(chips, cores, -1, HD)
    mine = lax.dynamic_index_in_dim(piece, core, 1, keepdims=False)
    other = lax.dynamic_index_in_dim(piece, 1 - core, 1, keepdims=False)
    other = lax.ppermute(other, "tp", [(t, t ^ 1) for t in range(shares)])
    both = jnp.stack([mine, other], axis=1)
    sheets = [
        [
            index(y, x, z) * shares + chip * cores + c
            for y in range(ys)
            for chip in range(chips)
            for z in range(ZS)
        ]
        for x in range(XS)
        for c in range(cores)
    ]
    flat = after(q.reshape(req * rows, HD), both)
    guests = [flat] + [move(flat, 0, s, 0) for s in range(1, XS)]
    whole = (ys, chips, ZS) + both.shape[1:]
    spread = jnp.broadcast_to(both[None, :, None], whole)
    prefix = lax.all_to_all(
        spread.reshape((-1,) + both.shape[1:]),
        ("inst", "tp"),
        split_axis=0,
        concat_axis=0,
        tiled=True,
        axis_index_groups=sheets,
    ).reshape(whole)
    ret = remote_partials(outbox.reshape(-1), pool, asked, rows)
    back = lax.all_to_all(after(ret, prefix, *guests), "inst", split_axis=0, concat_axis=0, tiled=True)
    past = prefix_partials(guests, prefix)
    past = [past[0]] + [move(past[s], 0, -s, 0) for s in range(1, XS)]
    merged = merge(me.reshape(1), slot_req, back, here)
    out = final(flags, merged, past)
    return out.reshape(req, steps, width)


def solution(mesh):
    placed = (
        P("inst", None, "tp"),
        P("inst", None, "tp"),
        P("inst", None, "tp"),
        P("inst", None),
        P("inst"),
        P("inst", None, None),
        P(("inst", "tp"), None),
        P(),
        P("inst"),
    )
    return jax.shard_map(
        per_device, mesh=mesh, in_specs=placed, out_specs=P("inst", None, "tp"), check_vma=False
    )
```

```python
import functools

import jax
import jax.numpy as jnp
from jax import lax
from jax.experimental import pallas as pl
from jax.experimental.pallas import tpu as pltpu
from jax.sharding import PartitionSpec as P

HD = 128
BLK = 128
CAP = 2
KEPT = 16
NEG = -1e30
XS = 4
ZS = 2
F32 = jnp.float32
BF16 = jnp.bfloat16

VMEM = pl.BlockSpec(memory_space=pltpu.VMEM)
SMEM = pl.BlockSpec(memory_space=pltpu.SMEM)


def params():
    return pltpu.CompilerParams(vmem_limit_bytes=16 * 1024 * 1024)


def cost(us):
    return pl.CostEstimate(flops=0, bytes_accessed=int(us * 3.0e6), transcendentals=0)


def dot_nt(a, b):
    return lax.dot_general(a, b, (((1,), (1,)), ((), ())), preferred_element_type=F32)


def dot_nn(a, b):
    return lax.dot_general(a, b, (((1,), (0,)), ((), ())), preferred_element_type=F32)


def with_ones(values):
    return jnp.concatenate([values, jnp.ones_like(values)], axis=1)


def batch_partials(jobs):
    rows = jobs[0][0].shape[0]
    scores = jnp.concatenate([dot_nt(q, keys) for q, keys, _, _ in jobs], axis=0) * (HD ** -0.5)
    masked = jobs[0][3] is not None
    if masked:
        valid = jnp.concatenate([job[3] for job in jobs], axis=0)
        scores = jnp.where(valid, scores, NEG)
    top = jnp.max(scores, axis=-1, keepdims=True)
    weights = jnp.exp(scores - top)
    if masked:
        weights = jnp.where(valid, weights, 0.0)
    weights = weights.astype(BF16)
    found = []
    for i, (_, _, values, _) in enumerate(jobs):
        both = dot_nn(weights[i * rows : (i + 1) * rows], with_ones(values))
        found.append((top[i * rows : (i + 1) * rows], both[:, HD:], both[:, :HD]))
    return found


def prep_kernel(pool_size, page, lens, local, slot_req, counts):
    for k in range(KEPT):
        for field in range(3):
            local[field, k] = 0

    def request(r, kept):
        length = lens[r]

        def block(j, kept):
            b = page[r, j]
            valid = jnp.minimum(length - j * BLK, BLK)
            away = b >= pool_size

            @pl.when(away)
            def _():
                slot_req[b - pool_size] = r
                counts[b - pool_size] = valid

            @pl.when(jnp.logical_not(away))
            def _():
                local[0, kept] = b
                local[1, kept] = r
                local[2, kept] = valid

            return kept + jnp.where(away, 0, 1)

        return lax.fori_loop(0, lax.shift_right_logical(length + BLK - 1, 7), block, kept)

    lax.fori_loop(0, lens.shape[0], request, 0)


def prep(page, lengths, pool_size, slots):
    return pl.pallas_call(
        functools.partial(prep_kernel, pool_size),
        out_shape=(
            jax.ShapeDtypeStruct((3, KEPT), jnp.int32),
            jax.ShapeDtypeStruct((slots,), jnp.int32),
            jax.ShapeDtypeStruct((slots,), jnp.int32),
        ),
        in_specs=[SMEM, SMEM],
        out_specs=(SMEM, SMEM, SMEM),
        compiler_params=params(),
        cost_estimate=cost(3),
        name="prep",
    )(page, lengths)


def pack_kernel(spots, slot_req, counts, hold, q, *refs):
    sources, pay = refs[:-1], refs[-1]
    rows = q.shape[1]
    body = CAP * rows
    upper = lax.broadcasted_iota(jnp.int32, (16, HD), 0) < 8
    tokens = sources[0].shape[0] // len(spots)
    most = sources[0].shape[1] // HD
    for d in range(len(spots)):
        for c in range(CAP):
            pay[d, c * rows : (c + 1) * rows, :] = q[slot_req[CAP * d + c]]
        tile = jnp.where(upper, counts[CAP * d], counts[CAP * d + 1])
        pay[d, body : body + 16, :] = tile.astype(F32).astype(BF16)
    for k, source in enumerate(sources):

        @pl.when(hold[0] == k)
        def _():
            for d, spot in enumerate(spots):
                for j in range(most):
                    at = body + 16 + j * tokens
                    col = (j % (source.shape[1] // HD)) * HD
                    pay[d, at : at + tokens, :] = source[
                        spot * tokens : (spot + 1) * tokens, col : col + HD
                    ]


def pack(spots, slot_req, counts, hold, q, columns):
    n = len(spots)
    rows = q.shape[1]
    held, wide = columns[0].shape
    height = CAP * rows + 16 + (wide // HD) * (held // n)
    return pl.pallas_call(
        functools.partial(pack_kernel, spots),
        out_shape=jax.ShapeDtypeStruct((n, height, HD), BF16),
        in_specs=[SMEM, SMEM, SMEM, VMEM] + [VMEM] * len(columns),
        out_specs=VMEM,
        compiler_params=params(),
        cost_estimate=cost(1.5),
        name="pack",
    )(slot_req, counts, hold, q, *columns)


def chip_of(position, core, chips):
    return (position + (chips // 2) * core) % chips


def gather_kernel(units, core, holders, asked, mine, other):
    chips, double, _ = mine.shape
    tokens = double // 2
    head = asked.shape[1] - units[0] * tokens
    found = [(k, j) for k, count in enumerate(units) for j in range(count)]
    for c in range(2):

        @pl.when(core[0] == c)
        def _():
            for out, parity in ((mine, c), (other, 1 - c)):
                for position in range(chips):
                    for part in range(2):
                        k, j = found[(chip_of(position, parity, chips) * 2 + parity) * 2 + part]
                        at = head + j * tokens
                        out[position, part * tokens : (part + 1) * tokens, :] = asked[
                            holders[k], at : at + tokens, :
                        ]


def gather(units, core, holders, asked, tokens):
    one = jax.ShapeDtypeStruct((sum(units) // 4, 2 * tokens, HD), BF16)
    return pl.pallas_call(
        functools.partial(gather_kernel, units),
        out_shape=(one, one),
        in_specs=[SMEM, SMEM, VMEM],
        out_specs=(VMEM, VMEM),
        compiler_params=params(),
        cost_estimate=cost(0.5),
        name="gather",
    )(core, holders, asked)


def remote_kernel(outbox, pool, pay, ret):
    n = pay.shape[0]
    rows = (ret.shape[1] - 8) // CAP
    each = BLK // rows
    lane = lax.broadcasted_iota(jnp.int32, (rows, BLK), 1)

    def group(g, carry):
        jobs = []
        for i in range(each):
            d = g * each + i
            marks = pay[d, CAP * rows : CAP * rows + 16, :].astype(F32).astype(jnp.int32)
            for c in range(CAP):
                kv = pool[outbox[d * CAP + c]]
                valid = lane < marks[8 * c : 8 * c + 1, :]
                jobs.append((pay[d, c * rows : (c + 1) * rows, :], kv[:, :HD], kv[:, HD:], valid))
        found = batch_partials(jobs)
        stats = []
        for i in range(each):
            stat = jnp.zeros((rows, BLK), F32)
            for c in range(CAP):
                top, total, out = found[i * CAP + c]
                ret[g * each + i, c * rows : (c + 1) * rows, :] = out
                stat = jnp.where(lane == 2 * c, top, stat)
                stat = jnp.where(lane == 2 * c + 1, total, stat)
            stats.append(stat)
        turned = jnp.concatenate(stats, axis=0).T[:8]
        for i in range(each):
            ret[g * each + i, CAP * rows : CAP * rows + 8, :] = turned
        return carry

    lax.fori_loop(0, n // each, group, 0)


def remote_partials(outbox, pool, pay, rows):
    n = pay.shape[0]
    return pl.pallas_call(
        remote_kernel,
        out_shape=jax.ShapeDtypeStruct((n, CAP * rows + 8, HD), F32),
        in_specs=[SMEM, VMEM, VMEM],
        out_specs=VMEM,
        compiler_params=params(),
        cost_estimate=cost(6),
        name="remote_partials",
    )(outbox, pool, pay)


def local_kernel(local, pool, q, fresh, out_o, out_m, out_l):
    req, rows, _ = q.shape
    steps = rows // 8
    keys = fresh.shape[1]
    step = lax.broadcasted_iota(jnp.int32, (rows, keys), 0) // 8
    place = lax.broadcasted_iota(jnp.int32, (rows, keys), 1)
    causal = (place <= step) & (place < steps)
    found = batch_partials([(q[r], fresh[r, :, :HD], fresh[r, :, HD:], causal) for r in range(req)])
    for r, (top, total, out) in enumerate(found):
        out_o[r] = out
        out_l[r] = total
        out_m[r] = jnp.broadcast_to(top, (rows, HD))
    lane = lax.broadcasted_iota(jnp.int32, (rows, BLK), 1)

    def batch(g, carry):
        jobs = []
        for i in range(8):
            k = g * 8 + i
            kv = pool[local[0, k]]
            jobs.append((q[local[1, k]], kv[:, :HD], kv[:, HD:], lane < local[2, k]))
        found = batch_partials(jobs)
        for i in range(8):
            r = local[1, g * 8 + i]
            top, total, out = found[i]
            old = out_m[r]
            new = jnp.maximum(old, top)
            keep, add = jnp.exp(old - new), jnp.exp(top - new)
            out_m[r] = new
            out_l[r] = out_l[r] * keep + total * add
            out_o[r] = out_o[r] * keep + out * add
        return carry

    lax.fori_loop(0, KEPT // 8, batch, 0)


def local_partials(local, pool, q, fresh):
    one = jax.ShapeDtypeStruct(q.shape, F32)
    return pl.pallas_call(
        local_kernel,
        out_shape=(one, one, one),
        in_specs=[SMEM, VMEM, VMEM, VMEM],
        out_specs=(VMEM, VMEM, VMEM),
        compiler_params=params(),
        cost_estimate=cost(6),
        name="local_partials",
    )(local, pool, q, fresh)


def prefix_kernel(q0, q1, q2, q3, kv, p0, p1, p2, p3, q, out_o, out_m, out_l):
    chips, cores, double = kv.shape[1], kv.shape[3], kv.shape[4]
    tokens = double // 2
    part = q0.shape[0]
    for s, source in enumerate((q0, q1, q2, q3)):
        q[s * part : (s + 1) * part, :] = source[...]
    out_o[...] = jnp.zeros_like(out_o)
    out_l[...] = jnp.zeros_like(out_l)
    out_m[...] = jnp.full_like(out_m, NEG)

    def pair(t, carry):
        jobs = []
        for b in range(cores):
            keys = kv[:, t, :, b, :tokens].reshape(BLK, HD)
            values = kv[:, t, :, b, tokens:].reshape(BLK, HD)
            jobs.append((q[...], keys, values, None))
        found = batch_partials(jobs)
        old = out_m[...]
        new = jnp.maximum(jnp.maximum(old, found[0][0]), found[1][0])
        keep = jnp.exp(old - new)
        acc_l, acc_o = out_l[...] * keep, out_o[...] * keep
        for top, total, out in found:
            add = jnp.exp(top - new)
            acc_l = acc_l + total * add
            acc_o = acc_o + out * add
        out_m[...] = new
        out_l[...] = acc_l
        out_o[...] = acc_o
        return carry

    lax.fori_loop(0, chips, pair, 0)
    lane = lax.broadcasted_iota(jnp.int32, (BLK, HD), 1)
    for s, target in enumerate((p0, p1, p2, p3)):
        target[:part, :] = out_o[s * part : (s + 1) * part, :]
        for k in range(part // BLK):
            at = s * part + k * BLK
            stat = jnp.where(lane == 0, out_m[at : at + BLK, :], out_l[at : at + BLK, :])
            target[part + 8 * k : part + 8 * k + 8, :] = stat.T[:8]


def prefix_partials(queries, kv):
    part = queries[0].shape[0]
    one = jax.ShapeDtypeStruct((part + 8 * (part // BLK), HD), F32)
    whole = pltpu.VMEM((XS * part, HD), F32)
    return pl.pallas_call(
        prefix_kernel,
        out_shape=(one,) * XS,
        in_specs=[VMEM] * (XS + 1),
        out_specs=(VMEM,) * XS,
        scratch_shapes=[pltpu.VMEM((XS * part, HD), BF16), whole, whole, whole],
        compiler_params=params(),
        cost_estimate=cost(6),
        name="prefix_partials",
    )(*queries, kv)


def merge_kernel(me, slot_req, ret, lo, lm, ll, acc, top, total, turned):
    req, rows, _ = lo.shape
    n = ret.shape[0]
    batch = min(16, n)
    body = CAP * rows
    per = BLK // rows
    for g in range(n // batch):
        turned[g] = ret[g * batch : (g + 1) * batch, body : body + 8, :].reshape(batch * 8, BLK).T
    mine = pl.multiple_of(lax.rem(me[0], per) * rows, rows)
    top[...] = lm[...]
    for g in range(n // batch):
        stats = turned[g, pl.ds(mine, rows), :]
        for i in range(batch):
            for c in range(CAP):
                r = slot_req[(g * batch + i) * CAP + c]
                col = 8 * i + 2 * c
                top[r] = jnp.maximum(top[r], stats[:, col : col + 1])
    for r in range(req):
        factor = jnp.exp(lm[r] - top[r])
        total[r] = ll[r] * factor
        acc[r] = lo[r] * factor
    for g in range(n // batch):
        stats = turned[g, pl.ds(mine, rows), :]
        for i in range(batch):
            for c in range(CAP):
                s = g * batch + i
                r = slot_req[s * CAP + c]
                col = 8 * i + 2 * c
                factor = jnp.exp(stats[:, col : col + 1] - top[r])
                total[r] += stats[:, col + 1 : col + 2] * factor
                acc[r] += ret[s, c * rows : (c + 1) * rows, :] * factor


def merge(me, slot_req, ret, here):
    n = ret.shape[0]
    batch = min(16, n)
    one = jax.ShapeDtypeStruct(here[0].shape, F32)
    return pl.pallas_call(
        merge_kernel,
        out_shape=(one, one, one),
        in_specs=[SMEM, SMEM] + [VMEM] * 4,
        out_specs=(VMEM, VMEM, VMEM),
        scratch_shapes=[pltpu.VMEM((n // batch, BLK, batch * 8), F32)],
        compiler_params=params(),
        cost_estimate=cost(2),
        name="merge",
    )(me, slot_req, ret, *here)


def final_kernel(flags, acc, top, total, p0, p1, p2, p3, out, past):
    req, rows, _ = acc.shape
    part = req * rows
    tiles = part // BLK
    per = BLK // rows
    parts = (p0, p1, p2, p3)
    past[...] = jnp.concatenate([p[part:, :] for p in parts], axis=0).T
    for r in range(req):
        use = flags[r] == 1
        at = (r % per) * rows
        tops, sums = [], []
        for p in range(XS):
            col = (p * tiles + r // per) * 8
            stat = past[at : at + rows, col : col + 2]
            tops.append(jnp.where(use, stat[:, 0:1], NEG))
            sums.append(stat[:, 1:2])
        peak = top[r]
        for found in tops:
            peak = jnp.maximum(peak, found)
        factor = jnp.exp(top[r] - peak)
        sum_l, sum_o = total[r] * factor, acc[r] * factor
        for p in range(XS):
            factor = jnp.exp(tops[p] - peak)
            sum_l = sum_l + sums[p] * factor
            sum_o = sum_o + parts[p][r * rows : (r + 1) * rows, :] * factor
        out[r] = (sum_o / sum_l).astype(BF16)


def final(flags, merged, past):
    req, rows, _ = merged[0].shape
    return pl.pallas_call(
        final_kernel,
        out_shape=jax.ShapeDtypeStruct((req, rows, HD), BF16),
        in_specs=[SMEM] + [VMEM] * (3 + XS),
        out_specs=VMEM,
        scratch_shapes=[pltpu.VMEM((BLK, XS * (req * rows // BLK) * 8), F32)],
        compiler_params=params(),
        cost_estimate=cost(1),
        name="final",
    )(flags, *merged, *past)


def after(value, *others):
    return lax.optimization_barrier((value, others))[0]


def per_device(queries, new_kv, pool, page, lengths, outbox, prefix_store, owner, flags):
    req, steps, width = queries.shape
    pool_size = pool.shape[0]
    rows = steps * (width // HD)
    n = lax.axis_size("inst")
    shares = lax.axis_size("tp")
    ys = n // (XS * ZS)
    plane = ys * ZS
    me = lax.axis_index("inst").astype(jnp.int32)
    owned = owner[0]

    def index(y, x, z):
        return ((y % ys) * XS + x % XS) * ZS + z % ZS

    def move(value, dy, dx, dz):
        pairs = [
            (index(y, x, z), index(y + dy, x + dx, z + dz))
            for y in range(ys)
            for x in range(XS)
            for z in range(ZS)
        ]
        return lax.ppermute(value, "inst", pairs)

    steps_out = (
        (3, 0, 0, 0),
        (3, 0, 0, 1),
        (3, 0, 1, 0),
        (3, 0, -1, 0),
        (2, 1, 0, 0),
        (2, -1, 0, 0),
    )
    columns = []
    holders = []
    first = 0
    for units, dy, dx, dz in steps_out:
        part = prefix_store[:, first * HD : (first + units) * HD]
        first += units
        columns.append(move(part, dy, dx, dz) if holders else part)
        holders.append(index(owned // (XS * ZS) + dy, owned // ZS + dx, owned + dz))
    hold = sum(jnp.where(me == holders[k], k, 0) for k in range(1, len(steps_out)))
    spots = [
        ((i // ZS) % XS) * plane + (i // (XS * ZS)) * ZS + i % ZS for i in range(n)
    ]

    q = queries.reshape(req, rows, HD)
    local, slot_req, counts = prep(page, lengths, pool_size, n * CAP)
    tokens = prefix_store.shape[0] // n
    tokens = prefix_store.shape[0] // n
    units = tuple(step[0] for step in steps_out)
    pay = pack(spots, slot_req, counts, hold.reshape(1), q, columns)
    asked = lax.all_to_all(pay, "inst", split_axis=0, concat_axis=0, tiled=True)
    fresh = jnp.pad(new_kv, ((0, 0), (0, 16 - steps), (0, 0)))
    here = local_partials(local, pool, q, fresh)

    cores = 2
    chips = shares // cores
    core = lax.axis_index("tp").astype(jnp.int32) % cores
    mine, other = gather(
        units, core.reshape(1), jnp.stack(holders).astype(jnp.int32), asked, tokens
    )
    other = lax.ppermute(after(other, *here), "tp", [(t, t ^ 1) for t in range(shares)])
    both = jnp.stack([mine, other], axis=1)
    sheets = [
        [
            index(y + (ys // 2) * c, x, z) * shares + chip_of(p, c, chips) * cores + c
            for y in range(ys)
            for p in range(chips)
            for z in range(ZS)
        ]
        for x in range(XS)
        for c in range(cores)
    ]
    flat = after(q.reshape(req * rows, HD), both)
    guests = [flat] + [move(flat, 0, s, 0) for s in range(1, XS)]
    whole = (ys, chips, ZS) + both.shape[1:]
    spread = jnp.broadcast_to(both[None, :, None], whole)
    prefix = lax.all_to_all(
        spread.reshape((-1,) + both.shape[1:]),
        ("inst", "tp"),
        split_axis=0,
        concat_axis=0,
        tiled=True,
        axis_index_groups=sheets,
    ).reshape(whole)
    ret = remote_partials(outbox.reshape(-1), pool, asked, rows)
    back = lax.all_to_all(after(ret, prefix, *guests), "inst", split_axis=0, concat_axis=0, tiled=True)
    past = prefix_partials(guests, prefix)
    past = [past[0]] + [move(past[s], 0, -s, 0) for s in range(1, XS)]
    merged = merge(me.reshape(1), slot_req, back, here)
    out = final(flags, merged, past)
    return out.reshape(req, steps, width)


def solution(mesh):
    placed = (
        P("inst", None, "tp"),
        P("inst", None, "tp"),
        P("inst", None, "tp"),
        P("inst", None),
        P("inst"),
        P("inst", None, None),
        P(("inst", "tp"), None),
        P(),
        P("inst"),
    )
    return jax.shard_map(
        per_device, mesh=mesh, in_specs=placed, out_specs=P("inst", None, "tp"), check_vma=False
    )
```

```python
import functools

import jax
import jax.numpy as jnp
from jax import lax
from jax.experimental import pallas as pl
from jax.experimental.pallas import tpu as pltpu
from jax.sharding import PartitionSpec as P

HD = 128
BLK = 128
CAP = 2
KEPT = 16
NEG = -1e30
XS = 4
ZS = 2
F32 = jnp.float32
BF16 = jnp.bfloat16

VMEM = pl.BlockSpec(memory_space=pltpu.VMEM)
SMEM = pl.BlockSpec(memory_space=pltpu.SMEM)


def params():
    return pltpu.CompilerParams(vmem_limit_bytes=16 * 1024 * 1024)


def cost(us):
    return pl.CostEstimate(flops=0, bytes_accessed=int(us * 3.0e6), transcendentals=0)


def dot_nt(a, b):
    return lax.dot_general(a, b, (((1,), (1,)), ((), ())), preferred_element_type=F32)


def dot_nn(a, b):
    return lax.dot_general(a, b, (((1,), (0,)), ((), ())), preferred_element_type=F32)


def with_ones(values):
    return jnp.concatenate([values, jnp.ones_like(values)], axis=1)


def batch_partials(jobs):
    rows = jobs[0][0].shape[0]
    scores = jnp.concatenate([dot_nt(q, keys) for q, keys, _, _ in jobs], axis=0) * (HD ** -0.5)
    masked = jobs[0][3] is not None
    if masked:
        valid = jnp.concatenate([job[3] for job in jobs], axis=0)
        scores = jnp.where(valid, scores, NEG)
    top = jnp.max(scores, axis=-1, keepdims=True)
    weights = jnp.exp(scores - top)
    if masked:
        weights = jnp.where(valid, weights, 0.0)
    weights = weights.astype(BF16)
    found = []
    for i, (_, _, values, _) in enumerate(jobs):
        both = dot_nn(weights[i * rows : (i + 1) * rows], with_ones(values))
        found.append((top[i * rows : (i + 1) * rows], both[:, HD:], both[:, :HD]))
    return found


def prep_kernel(pool_size, page, lens, local, slot_req, counts):
    for k in range(KEPT):
        for field in range(3):
            local[field, k] = 0

    def request(r, kept):
        length = lens[r]

        def block(j, kept):
            b = page[r, j]
            valid = jnp.minimum(length - j * BLK, BLK)
            away = b >= pool_size

            @pl.when(away)
            def _():
                slot_req[b - pool_size] = r
                counts[b - pool_size] = valid

            @pl.when(jnp.logical_not(away))
            def _():
                local[0, kept] = b
                local[1, kept] = r
                local[2, kept] = valid

            return kept + jnp.where(away, 0, 1)

        return lax.fori_loop(0, lax.shift_right_logical(length + BLK - 1, 7), block, kept)

    lax.fori_loop(0, lens.shape[0], request, 0)


def prep(page, lengths, pool_size, slots):
    return pl.pallas_call(
        functools.partial(prep_kernel, pool_size),
        out_shape=(
            jax.ShapeDtypeStruct((3, KEPT), jnp.int32),
            jax.ShapeDtypeStruct((slots,), jnp.int32),
            jax.ShapeDtypeStruct((slots,), jnp.int32),
        ),
        in_specs=[SMEM, SMEM],
        out_specs=(SMEM, SMEM, SMEM),
        compiler_params=params(),
        cost_estimate=cost(3),
        name="prep",
    )(page, lengths)


def pack_kernel(spots, slot_req, counts, hold, q, *refs):
    sources, (pay, made, sems) = refs[:-3], refs[-3:]
    rows = q.shape[1]
    body = CAP * rows
    upper = lax.broadcasted_iota(jnp.int32, (16, HD), 0) < 8
    tokens = sources[0].shape[0] // len(spots)
    most = sources[0].shape[1] // HD
    groups = sems.shape[0]
    each = len(spots) // groups
    copies = []
    for g in range(groups):
        members = range(g * each, (g + 1) * each)
        for d in members:
            for c in range(CAP):
                made[d, c * rows : (c + 1) * rows, :] = q[slot_req[CAP * d + c]]
            tile = jnp.where(upper, counts[CAP * d], counts[CAP * d + 1])
            made[d, body : body + 16, :] = tile.astype(F32).astype(BF16)
        for k, source in enumerate(sources):

            @pl.when(hold[0] == k)
            def _():
                for d in members:
                    for j in range(most):
                        at = body + 16 + j * tokens
                        col = (j % (source.shape[1] // HD)) * HD
                        made[d, at : at + tokens, :] = source[
                            spots[d] * tokens : (spots[d] + 1) * tokens, col : col + HD
                        ]

        part = pl.ds(g * each, each)
        copies.append(pltpu.make_async_copy(made.at[part], pay.at[part], sems.at[g]))
        copies[-1].start()
    for copy in copies:
        copy.wait()


def pack(spots, slot_req, counts, hold, q, columns):
    n = len(spots)
    rows = q.shape[1]
    held, wide = columns[0].shape
    shape = (n, CAP * rows + 16 + (wide // HD) * (held // n), HD)
    return pl.pallas_call(
        functools.partial(pack_kernel, spots),
        out_shape=jax.ShapeDtypeStruct(shape, BF16),
        in_specs=[SMEM, SMEM, SMEM, VMEM] + [VMEM] * len(columns),
        out_specs=pl.BlockSpec(memory_space=pl.ANY),
        scratch_shapes=[pltpu.VMEM(shape, BF16), pltpu.SemaphoreType.DMA((4,))],
        compiler_params=params(),
        cost_estimate=cost(1.5),
        name="pack",
    )(slot_req, counts, hold, q, *columns)


def chip_of(position, core, chips):
    return (position + (chips // 2) * core) % chips


def gather_kernel(units, core, holders, asked, mine, other):
    chips, double, _ = mine.shape
    tokens = double // 2
    head = asked.shape[1] - units[0] * tokens
    found = [(k, j) for k, count in enumerate(units) for j in range(count)]
    for c in range(2):

        @pl.when(core[0] == c)
        def _():
            for out, parity in ((mine, c), (other, 1 - c)):
                for position in range(chips):
                    for part in range(2):
                        k, j = found[(chip_of(position, parity, chips) * 2 + parity) * 2 + part]
                        at = head + j * tokens
                        out[position, part * tokens : (part + 1) * tokens, :] = asked[
                            holders[k], at : at + tokens, :
                        ]


def gather(units, core, holders, asked, tokens):
    one = jax.ShapeDtypeStruct((sum(units) // 4, 2 * tokens, HD), BF16)
    return pl.pallas_call(
        functools.partial(gather_kernel, units),
        out_shape=(one, one),
        in_specs=[SMEM, SMEM, VMEM],
        out_specs=(VMEM, VMEM),
        compiler_params=params(),
        cost_estimate=cost(0.5),
        name="gather",
    )(core, holders, asked)


def remote_kernel(outbox, pool, pay, ret):
    n = pay.shape[0]
    rows = (ret.shape[1] - 8) // CAP
    each = BLK // rows
    lane = lax.broadcasted_iota(jnp.int32, (rows, BLK), 1)

    def group(g, carry):
        jobs = []
        for i in range(each):
            d = g * each + i
            marks = pay[d, CAP * rows : CAP * rows + 16, :].astype(F32).astype(jnp.int32)
            for c in range(CAP):
                kv = pool[outbox[d * CAP + c]]
                valid = lane < marks[8 * c : 8 * c + 1, :]
                jobs.append((pay[d, c * rows : (c + 1) * rows, :], kv[:, :HD], kv[:, HD:], valid))
        found = batch_partials(jobs)
        stats = []
        for i in range(each):
            stat = jnp.zeros((rows, BLK), F32)
            for c in range(CAP):
                top, total, out = found[i * CAP + c]
                ret[g * each + i, c * rows : (c + 1) * rows, :] = out
                stat = jnp.where(lane == 2 * c, top, stat)
                stat = jnp.where(lane == 2 * c + 1, total, stat)
            stats.append(stat)
        turned = jnp.concatenate(stats, axis=0).T[:8]
        for i in range(each):
            ret[g * each + i, CAP * rows : CAP * rows + 8, :] = turned
        return carry

    lax.fori_loop(0, n // each, group, 0)


def remote_partials(outbox, pool, pay, rows):
    n = pay.shape[0]
    return pl.pallas_call(
        remote_kernel,
        out_shape=jax.ShapeDtypeStruct((n, CAP * rows + 8, HD), F32),
        in_specs=[SMEM, VMEM, VMEM],
        out_specs=VMEM,
        compiler_params=params(),
        cost_estimate=cost(6),
        name="remote_partials",
    )(outbox, pool, pay)


def local_kernel(local, pool, q, fresh, out_o, out_m, out_l):
    req, rows, _ = q.shape
    steps = rows // 8
    keys = fresh.shape[1]
    step = lax.broadcasted_iota(jnp.int32, (rows, keys), 0) // 8
    place = lax.broadcasted_iota(jnp.int32, (rows, keys), 1)
    causal = (place <= step) & (place < steps)
    found = batch_partials([(q[r], fresh[r, :, :HD], fresh[r, :, HD:], causal) for r in range(req)])
    for r, (top, total, out) in enumerate(found):
        out_o[r] = out
        out_l[r] = total
        out_m[r] = jnp.broadcast_to(top, (rows, HD))
    lane = lax.broadcasted_iota(jnp.int32, (rows, BLK), 1)

    def batch(g, carry):
        jobs = []
        for i in range(8):
            k = g * 8 + i
            kv = pool[local[0, k]]
            jobs.append((q[local[1, k]], kv[:, :HD], kv[:, HD:], lane < local[2, k]))
        found = batch_partials(jobs)
        for i in range(8):
            r = local[1, g * 8 + i]
            top, total, out = found[i]
            old = out_m[r]
            new = jnp.maximum(old, top)
            keep, add = jnp.exp(old - new), jnp.exp(top - new)
            out_m[r] = new
            out_l[r] = out_l[r] * keep + total * add
            out_o[r] = out_o[r] * keep + out * add
        return carry

    lax.fori_loop(0, KEPT // 8, batch, 0)


def local_partials(local, pool, q, fresh):
    one = jax.ShapeDtypeStruct(q.shape, F32)
    return pl.pallas_call(
        local_kernel,
        out_shape=(one, one, one),
        in_specs=[SMEM, VMEM, VMEM, VMEM],
        out_specs=(VMEM, VMEM, VMEM),
        compiler_params=params(),
        cost_estimate=cost(6),
        name="local_partials",
    )(local, pool, q, fresh)


def prefix_kernel(count, *refs):
    sources, kv, targets = refs[:count], refs[count], refs[count + 1 : 2 * count + 1]
    q, out_o, out_m, out_l = refs[2 * count + 1 :]
    chips, cores, double = kv.shape[1], kv.shape[3], kv.shape[4]
    tokens = double // 2
    part = sources[0].shape[0]
    for s, source in enumerate(sources):
        q[s * part : (s + 1) * part, :] = source[...]
    out_o[...] = jnp.zeros_like(out_o)
    out_l[...] = jnp.zeros_like(out_l)
    out_m[...] = jnp.full_like(out_m, NEG)

    def pair(t, carry):
        jobs = []
        for b in range(cores):
            keys = kv[:, t, :, b, :tokens].reshape(BLK, HD)
            values = kv[:, t, :, b, tokens:].reshape(BLK, HD)
            jobs.append((q[...], keys, values, None))
        found = batch_partials(jobs)
        old = out_m[...]
        new = jnp.maximum(jnp.maximum(old, found[0][0]), found[1][0])
        keep = jnp.exp(old - new)
        acc_l, acc_o = out_l[...] * keep, out_o[...] * keep
        for top, total, out in found:
            add = jnp.exp(top - new)
            acc_l = acc_l + total * add
            acc_o = acc_o + out * add
        out_m[...] = new
        out_l[...] = acc_l
        out_o[...] = acc_o
        return carry

    lax.fori_loop(0, chips, pair, 0)
    lane = lax.broadcasted_iota(jnp.int32, (BLK, HD), 1)
    for s, target in enumerate(targets):
        target[:part, :] = out_o[s * part : (s + 1) * part, :]
        for k in range(part // BLK):
            at = s * part + k * BLK
            stat = jnp.where(lane == 0, out_m[at : at + BLK, :], out_l[at : at + BLK, :])
            target[part + 8 * k : part + 8 * k + 8, :] = stat.T[:8]


def prefix_partials(queries, kv):
    part = queries[0].shape[0]
    one = jax.ShapeDtypeStruct((part + 8 * (part // BLK), HD), F32)
    whole = pltpu.VMEM((len(queries) * part, HD), F32)
    return pl.pallas_call(
        functools.partial(prefix_kernel, len(queries)),
        out_shape=(one,) * len(queries),
        in_specs=[VMEM] * (len(queries) + 1),
        out_specs=(VMEM,) * len(queries),
        scratch_shapes=[pltpu.VMEM((len(queries) * part, HD), BF16), whole, whole, whole],
        compiler_params=params(),
        cost_estimate=cost(len(queries)),
        name="prefix_partials",
    )(*queries, kv)


def merge_kernel(me, slot_req, ret, lo, lm, ll, acc, top, total, turned):
    req, rows, _ = lo.shape
    n = ret.shape[0]
    batch = min(16, n)
    body = CAP * rows
    per = BLK // rows
    for g in range(n // batch):
        turned[g] = ret[g * batch : (g + 1) * batch, body : body + 8, :].reshape(batch * 8, BLK).T
    mine = pl.multiple_of(lax.rem(me[0], per) * rows, rows)
    top[...] = lm[...]
    for g in range(n // batch):
        stats = turned[g, pl.ds(mine, rows), :]
        for i in range(batch):
            for c in range(CAP):
                r = slot_req[(g * batch + i) * CAP + c]
                col = 8 * i + 2 * c
                top[r] = jnp.maximum(top[r], stats[:, col : col + 1])
    for r in range(req):
        factor = jnp.exp(lm[r] - top[r])
        total[r] = ll[r] * factor
        acc[r] = lo[r] * factor
    for g in range(n // batch):
        stats = turned[g, pl.ds(mine, rows), :]
        for i in range(batch):
            for c in range(CAP):
                s = g * batch + i
                r = slot_req[s * CAP + c]
                col = 8 * i + 2 * c
                factor = jnp.exp(stats[:, col : col + 1] - top[r])
                total[r] += stats[:, col + 1 : col + 2] * factor
                acc[r] += ret[s, c * rows : (c + 1) * rows, :] * factor


def merge(me, slot_req, ret, here):
    n = ret.shape[0]
    batch = min(16, n)
    one = jax.ShapeDtypeStruct(here[0].shape, F32)
    return pl.pallas_call(
        merge_kernel,
        out_shape=(one, one, one),
        in_specs=[SMEM, SMEM] + [VMEM] * 4,
        out_specs=(VMEM, VMEM, VMEM),
        scratch_shapes=[pltpu.VMEM((n // batch, BLK, batch * 8), F32)],
        compiler_params=params(),
        cost_estimate=cost(2),
        name="merge",
    )(me, slot_req, ret, *here)


def final_kernel(flags, acc, top, total, p0, p1, p2, p3, out, past):
    req, rows, _ = acc.shape
    part = req * rows
    tiles = part // BLK
    per = BLK // rows
    parts = (p0, p1, p2, p3)
    past[...] = jnp.concatenate([p[part:, :] for p in parts], axis=0).T
    for r in range(req):
        use = flags[r] == 1
        at = (r % per) * rows
        tops, sums = [], []
        for p in range(XS):
            col = (p * tiles + r // per) * 8
            stat = past[at : at + rows, col : col + 2]
            tops.append(jnp.where(use, stat[:, 0:1], NEG))
            sums.append(stat[:, 1:2])
        peak = top[r]
        for found in tops:
            peak = jnp.maximum(peak, found)
        factor = jnp.exp(top[r] - peak)
        sum_l, sum_o = total[r] * factor, acc[r] * factor
        for p in range(XS):
            factor = jnp.exp(tops[p] - peak)
            sum_l = sum_l + sums[p] * factor
            sum_o = sum_o + parts[p][r * rows : (r + 1) * rows, :] * factor
        out[r] = (sum_o / sum_l).astype(BF16)


def final(flags, merged, past):
    req, rows, _ = merged[0].shape
    return pl.pallas_call(
        final_kernel,
        out_shape=jax.ShapeDtypeStruct((req, rows, HD), BF16),
        in_specs=[SMEM] + [VMEM] * (3 + XS),
        out_specs=VMEM,
        scratch_shapes=[pltpu.VMEM((BLK, XS * (req * rows // BLK) * 8), F32)],
        compiler_params=params(),
        cost_estimate=cost(1),
        name="final",
    )(flags, *merged, *past)


def after(value, *others):
    return lax.optimization_barrier((value, others))[0]


def per_device(queries, new_kv, pool, page, lengths, outbox, prefix_store, owner, flags):
    req, steps, width = queries.shape
    pool_size = pool.shape[0]
    rows = steps * (width // HD)
    n = lax.axis_size("inst")
    shares = lax.axis_size("tp")
    ys = n // (XS * ZS)
    plane = ys * ZS
    me = lax.axis_index("inst").astype(jnp.int32)
    owned = owner[0]

    def index(y, x, z):
        return ((y % ys) * XS + x % XS) * ZS + z % ZS

    def move(value, dy, dx, dz):
        pairs = [
            (index(y, x, z), index(y + dy, x + dx, z + dz))
            for y in range(ys)
            for x in range(XS)
            for z in range(ZS)
        ]
        return lax.ppermute(value, "inst", pairs)

    steps_out = (
        (3, 0, 0, 0),
        (3, 0, 0, 1),
        (3, 0, 1, 0),
        (3, 0, -1, 0),
        (2, 1, 0, 0),
        (2, -1, 0, 0),
    )
    columns = []
    holders = []
    first = 0
    for units, dy, dx, dz in steps_out:
        part = prefix_store[:, first * HD : (first + units) * HD]
        first += units
        columns.append(move(part, dy, dx, dz) if holders else part)
        holders.append(index(owned // (XS * ZS) + dy, owned // ZS + dx, owned + dz))
    hold = sum(jnp.where(me == holders[k], k, 0) for k in range(1, len(steps_out)))
    spots = [
        ((i // ZS) % XS) * plane + (i // (XS * ZS)) * ZS + i % ZS for i in range(n)
    ]

    q = queries.reshape(req, rows, HD)
    local, slot_req, counts = prep(page, lengths, pool_size, n * CAP)
    tokens = prefix_store.shape[0] // n
    tokens = prefix_store.shape[0] // n
    units = tuple(step[0] for step in steps_out)
    pay = pack(spots, slot_req, counts, hold.reshape(1), q, columns)
    asked = lax.all_to_all(pay, "inst", split_axis=0, concat_axis=0, tiled=True)
    fresh = jnp.pad(new_kv, ((0, 0), (0, 16 - steps), (0, 0)))
    here = local_partials(local, pool, q, fresh)

    cores = 2
    chips = shares // cores
    core = lax.axis_index("tp").astype(jnp.int32) % cores
    mine, other = gather(
        units, core.reshape(1), jnp.stack(holders).astype(jnp.int32), asked, tokens
    )
    other = lax.ppermute(after(other, *here), "tp", [(t, t ^ 1) for t in range(shares)])
    both = jnp.stack([mine, other], axis=1)
    sheets = [
        [
            index(y + (ys // 2) * c, x, z) * shares + chip_of(p, c, chips) * cores + c
            for y in range(ys)
            for p in range(chips)
            for z in range(ZS)
        ]
        for x in range(XS)
        for c in range(cores)
    ]
    flat = after(q.reshape(req * rows, HD), both)
    guests = [flat] + [move(flat, 0, s, 0) for s in range(1, XS)]
    whole = (ys, chips, ZS) + both.shape[1:]
    spread = jnp.broadcast_to(both[None, :, None], whole)
    prefix = lax.all_to_all(
        spread.reshape((-1,) + both.shape[1:]),
        ("inst", "tp"),
        split_axis=0,
        concat_axis=0,
        tiled=True,
        axis_index_groups=sheets,
    ).reshape(whole)
    ret = remote_partials(outbox.reshape(-1), pool, asked, rows)
    back = lax.all_to_all(after(ret, prefix, *guests), "inst", split_axis=0, concat_axis=0, tiled=True)
    past = prefix_partials(guests[1:], prefix)
    sent = [move(past[s - 1], 0, -s, 0) for s in range(1, XS)]
    own = prefix_partials([after(flat, past[0])], prefix)
    past = [own[0]] + sent
    merged = merge(me.reshape(1), slot_req, back, here)
    out = final(flags, merged, past)
    return out.reshape(req, steps, width)


def solution(mesh):
    placed = (
        P("inst", None, "tp"),
        P("inst", None, "tp"),
        P("inst", None, "tp"),
        P("inst", None),
        P("inst"),
        P("inst", None, None),
        P(("inst", "tp"), None),
        P(),
        P("inst"),
    )
    return jax.shard_map(
        per_device, mesh=mesh, in_specs=placed, out_specs=P("inst", None, "tp"), check_vma=False
    )
```

```python
import functools

import jax
import jax.numpy as jnp
from jax import lax
from jax.experimental import pallas as pl
from jax.experimental.pallas import tpu as pltpu
from jax.sharding import PartitionSpec as P

HD = 128
BLK = 128
CAP = 2
KEPT = 16
NEG = -1e30
XS = 4
ZS = 2
F32 = jnp.float32
BF16 = jnp.bfloat16

VMEM = pl.BlockSpec(memory_space=pltpu.VMEM)
SMEM = pl.BlockSpec(memory_space=pltpu.SMEM)


def params():
    return pltpu.CompilerParams(vmem_limit_bytes=16 * 1024 * 1024)


def cost(us):
    return pl.CostEstimate(flops=0, bytes_accessed=int(us * 3.0e6), transcendentals=0)


def dot_nt(a, b):
    return lax.dot_general(a, b, (((1,), (1,)), ((), ())), preferred_element_type=F32)


def dot_nn(a, b):
    return lax.dot_general(a, b, (((1,), (0,)), ((), ())), preferred_element_type=F32)


def with_ones(values):
    return jnp.concatenate([values, jnp.ones_like(values)], axis=1)


def batch_partials(jobs):
    rows = jobs[0][0].shape[0]
    scores = jnp.concatenate([dot_nt(q, keys) for q, keys, _, _ in jobs], axis=0) * (HD ** -0.5)
    masked = jobs[0][3] is not None
    if masked:
        valid = jnp.concatenate([job[3] for job in jobs], axis=0)
        scores = jnp.where(valid, scores, NEG)
    top = jnp.max(scores, axis=-1, keepdims=True)
    weights = jnp.exp(scores - top)
    if masked:
        weights = jnp.where(valid, weights, 0.0)
    weights = weights.astype(BF16)
    found = []
    for i, (_, _, values, _) in enumerate(jobs):
        both = dot_nn(weights[i * rows : (i + 1) * rows], with_ones(values))
        found.append((top[i * rows : (i + 1) * rows], both[:, HD:], both[:, :HD]))
    return found


def prep_kernel(pool_size, page, lens, local, slot_req, counts):
    for k in range(KEPT):
        for field in range(3):
            local[field, k] = 0

    def request(r, kept):
        length = lens[r]

        def block(j, kept):
            b = page[r, j]
            valid = jnp.minimum(length - j * BLK, BLK)
            away = b >= pool_size

            @pl.when(away)
            def _():
                slot_req[b - pool_size] = r
                counts[b - pool_size] = valid

            @pl.when(jnp.logical_not(away))
            def _():
                local[0, kept] = b
                local[1, kept] = r
                local[2, kept] = valid

            return kept + jnp.where(away, 0, 1)

        return lax.fori_loop(0, lax.shift_right_logical(length + BLK - 1, 7), block, kept)

    lax.fori_loop(0, lens.shape[0], request, 0)


def prep(page, lengths, pool_size, slots):
    return pl.pallas_call(
        functools.partial(prep_kernel, pool_size),
        out_shape=(
            jax.ShapeDtypeStruct((3, KEPT), jnp.int32),
            jax.ShapeDtypeStruct((slots,), jnp.int32),
            jax.ShapeDtypeStruct((slots,), jnp.int32),
        ),
        in_specs=[SMEM, SMEM],
        out_specs=(SMEM, SMEM, SMEM),
        compiler_params=params(),
        cost_estimate=cost(3),
        name="prep",
    )(page, lengths)


def pack_kernel(spots, slot_req, counts, hold, q, *refs):
    sources, (pay, made, sems) = refs[:-3], refs[-3:]
    rows = q.shape[1]
    body = CAP * rows
    upper = lax.broadcasted_iota(jnp.int32, (16, HD), 0) < 8
    tokens = sources[0].shape[0] // len(spots)
    most = sources[0].shape[1] // HD
    groups = sems.shape[0]
    each = len(spots) // groups
    copies = []
    for g in range(groups):
        members = range(g * each, (g + 1) * each)
        for d in members:
            for c in range(CAP):
                made[d, c * rows : (c + 1) * rows, :] = q[slot_req[CAP * d + c]]
            tile = jnp.where(upper, counts[CAP * d], counts[CAP * d + 1])
            made[d, body : body + 16, :] = tile.astype(F32).astype(BF16)
        for k, source in enumerate(sources):

            @pl.when(hold[0] == k)
            def _():
                for d in members:
                    for j in range(most):
                        at = body + 16 + j * tokens
                        col = (j % (source.shape[1] // HD)) * HD
                        made[d, at : at + tokens, :] = source[
                            spots[d] * tokens : (spots[d] + 1) * tokens, col : col + HD
                        ]

        part = pl.ds(g * each, each)
        copies.append(pltpu.make_async_copy(made.at[part], pay.at[part], sems.at[g]))
        copies[-1].start()
    for copy in copies:
        copy.wait()


def pack(spots, slot_req, counts, hold, q, columns):
    n = len(spots)
    rows = q.shape[1]
    held, wide = columns[0].shape
    shape = (n, CAP * rows + 16 + (wide // HD) * (held // n), HD)
    return pl.pallas_call(
        functools.partial(pack_kernel, spots),
        out_shape=jax.ShapeDtypeStruct(shape, BF16),
        in_specs=[SMEM, SMEM, SMEM, VMEM] + [VMEM] * len(columns),
        out_specs=pl.BlockSpec(memory_space=pl.ANY),
        scratch_shapes=[pltpu.VMEM(shape, BF16), pltpu.SemaphoreType.DMA((4,))],
        compiler_params=params(),
        cost_estimate=cost(1.5),
        name="pack",
    )(slot_req, counts, hold, q, *columns)


def chip_of(position, core, chips):
    return (position + (chips // 2) * core) % chips


def gather_kernel(units, core, holders, asked, mine, other):
    chips, double, _ = mine.shape
    tokens = double // 2
    head = asked.shape[1] - units[0] * tokens
    found = [(k, j) for k, count in enumerate(units) for j in range(count)]
    for c in range(2):

        @pl.when(core[0] == c)
        def _():
            for out, parity in ((mine, c), (other, 1 - c)):
                for position in range(chips):
                    for part in range(2):
                        k, j = found[(chip_of(position, parity, chips) * 2 + parity) * 2 + part]
                        at = head + j * tokens
                        out[position, part * tokens : (part + 1) * tokens, :] = asked[
                            holders[k], at : at + tokens, :
                        ]


def gather(units, core, holders, asked, tokens):
    one = jax.ShapeDtypeStruct((sum(units) // 4, 2 * tokens, HD), BF16)
    return pl.pallas_call(
        functools.partial(gather_kernel, units),
        out_shape=(one, one),
        in_specs=[SMEM, SMEM, VMEM],
        out_specs=(VMEM, VMEM),
        compiler_params=params(),
        cost_estimate=cost(0.5),
        name="gather",
    )(core, holders, asked)


def remote_kernel(outbox, pool, pay, back, ret, sems):
    n = pay.shape[0]
    rows = (ret.shape[1] - 8) // CAP
    each = BLK // rows
    lane = lax.broadcasted_iota(jnp.int32, (rows, BLK), 1)

    def group(g, carry):
        jobs = []
        for i in range(each):
            d = g * each + i
            marks = pay[d, CAP * rows : CAP * rows + 16, :].astype(F32).astype(jnp.int32)
            for c in range(CAP):
                kv = pool[outbox[d * CAP + c]]
                valid = lane < marks[8 * c : 8 * c + 1, :]
                jobs.append((pay[d, c * rows : (c + 1) * rows, :], kv[:, :HD], kv[:, HD:], valid))
        found = batch_partials(jobs)
        stats = []
        for i in range(each):
            stat = jnp.zeros((rows, BLK), F32)
            for c in range(CAP):
                top, total, out = found[i * CAP + c]
                ret[g * each + i, c * rows : (c + 1) * rows, :] = out
                stat = jnp.where(lane == 2 * c, top, stat)
                stat = jnp.where(lane == 2 * c + 1, total, stat)
            stats.append(stat)
        turned = jnp.concatenate(stats, axis=0).T[:8]
        for i in range(each):
            ret[g * each + i, CAP * rows : CAP * rows + 8, :] = turned
        leave(g).start()
        return carry

    def leave(g):
        part = pl.ds(g * each, each)
        return pltpu.make_async_copy(ret.at[part], back.at[part], sems.at[g])

    def left(g, carry):
        leave(g).wait()
        return carry

    lax.fori_loop(0, n // each, group, 0)
    lax.fori_loop(0, n // each, left, 0)


def remote_partials(outbox, pool, pay, rows):
    n = pay.shape[0]
    shape = (n, CAP * rows + 8, HD)
    return pl.pallas_call(
        remote_kernel,
        out_shape=jax.ShapeDtypeStruct(shape, F32),
        in_specs=[SMEM, VMEM, VMEM],
        out_specs=pl.BlockSpec(memory_space=pl.ANY),
        scratch_shapes=[pltpu.VMEM(shape, F32), pltpu.SemaphoreType.DMA((n * rows // BLK,))],
        compiler_params=params(),
        cost_estimate=cost(6),
        name="remote_partials",
    )(outbox, pool, pay)


def local_kernel(local, pool, q, fresh, out_o, out_m, out_l):
    req, rows, _ = q.shape
    steps = rows // 8
    keys = fresh.shape[1]
    step = lax.broadcasted_iota(jnp.int32, (rows, keys), 0) // 8
    place = lax.broadcasted_iota(jnp.int32, (rows, keys), 1)
    causal = (place <= step) & (place < steps)
    found = batch_partials([(q[r], fresh[r, :, :HD], fresh[r, :, HD:], causal) for r in range(req)])
    for r, (top, total, out) in enumerate(found):
        out_o[r] = out
        out_l[r] = total
        out_m[r] = jnp.broadcast_to(top, (rows, HD))
    lane = lax.broadcasted_iota(jnp.int32, (rows, BLK), 1)

    def batch(g, carry):
        jobs = []
        for i in range(8):
            k = g * 8 + i
            kv = pool[local[0, k]]
            jobs.append((q[local[1, k]], kv[:, :HD], kv[:, HD:], lane < local[2, k]))
        found = batch_partials(jobs)
        for i in range(8):
            r = local[1, g * 8 + i]
            top, total, out = found[i]
            old = out_m[r]
            new = jnp.maximum(old, top)
            keep, add = jnp.exp(old - new), jnp.exp(top - new)
            out_m[r] = new
            out_l[r] = out_l[r] * keep + total * add
            out_o[r] = out_o[r] * keep + out * add
        return carry

    lax.fori_loop(0, KEPT // 8, batch, 0)


def local_partials(local, pool, q, fresh):
    one = jax.ShapeDtypeStruct(q.shape, F32)
    return pl.pallas_call(
        local_kernel,
        out_shape=(one, one, one),
        in_specs=[SMEM, VMEM, VMEM, VMEM],
        out_specs=(VMEM, VMEM, VMEM),
        compiler_params=params(),
        cost_estimate=cost(6),
        name="local_partials",
    )(local, pool, q, fresh)


def prefix_kernel(count, *refs):
    sources, kv, targets = refs[:count], refs[count], refs[count + 1 : 2 * count + 1]
    q, out_o, out_m, out_l = refs[2 * count + 1 :]
    chips, cores, double = kv.shape[1], kv.shape[3], kv.shape[4]
    tokens = double // 2
    part = sources[0].shape[0]
    for s, source in enumerate(sources):
        q[s * part : (s + 1) * part, :] = source[...]
    out_o[...] = jnp.zeros_like(out_o)
    out_l[...] = jnp.zeros_like(out_l)
    out_m[...] = jnp.full_like(out_m, NEG)

    def pair(t, carry):
        jobs = []
        for b in range(cores):
            keys = kv[:, t, :, b, :tokens].reshape(BLK, HD)
            values = kv[:, t, :, b, tokens:].reshape(BLK, HD)
            jobs.append((q[...], keys, values, None))
        found = batch_partials(jobs)
        old = out_m[...]
        new = jnp.maximum(jnp.maximum(old, found[0][0]), found[1][0])
        keep = jnp.exp(old - new)
        acc_l, acc_o = out_l[...] * keep, out_o[...] * keep
        for top, total, out in found:
            add = jnp.exp(top - new)
            acc_l = acc_l + total * add
            acc_o = acc_o + out * add
        out_m[...] = new
        out_l[...] = acc_l
        out_o[...] = acc_o
        return carry

    lax.fori_loop(0, chips, pair, 0)
    lane = lax.broadcasted_iota(jnp.int32, (BLK, HD), 1)
    for s, target in enumerate(targets):
        target[:part, :] = out_o[s * part : (s + 1) * part, :]
        for k in range(part // BLK):
            at = s * part + k * BLK
            stat = jnp.where(lane == 0, out_m[at : at + BLK, :], out_l[at : at + BLK, :])
            target[part + 8 * k : part + 8 * k + 8, :] = stat.T[:8]


def prefix_partials(queries, kv):
    part = queries[0].shape[0]
    one = jax.ShapeDtypeStruct((part + 8 * (part // BLK), HD), F32)
    whole = pltpu.VMEM((len(queries) * part, HD), F32)
    return pl.pallas_call(
        functools.partial(prefix_kernel, len(queries)),
        out_shape=(one,) * len(queries),
        in_specs=[VMEM] * (len(queries) + 1),
        out_specs=(VMEM,) * len(queries),
        scratch_shapes=[pltpu.VMEM((len(queries) * part, HD), BF16), whole, whole, whole],
        compiler_params=params(),
        cost_estimate=cost(len(queries)),
        name="prefix_partials",
    )(*queries, kv)


def merge_kernel(me, slot_req, ret, lo, lm, ll, acc, top, total, turned):
    req, rows, _ = lo.shape
    n = ret.shape[0]
    batch = min(16, n)
    body = CAP * rows
    per = BLK // rows
    for g in range(n // batch):
        turned[g] = ret[g * batch : (g + 1) * batch, body : body + 8, :].reshape(batch * 8, BLK).T
    mine = pl.multiple_of(lax.rem(me[0], per) * rows, rows)
    top[...] = lm[...]
    for g in range(n // batch):
        stats = turned[g, pl.ds(mine, rows), :]
        for i in range(batch):
            for c in range(CAP):
                r = slot_req[(g * batch + i) * CAP + c]
                col = 8 * i + 2 * c
                top[r] = jnp.maximum(top[r], stats[:, col : col + 1])
    for r in range(req):
        factor = jnp.exp(lm[r] - top[r])
        total[r] = ll[r] * factor
        acc[r] = lo[r] * factor
    for g in range(n // batch):
        stats = turned[g, pl.ds(mine, rows), :]
        for i in range(batch):
            for c in range(CAP):
                s = g * batch + i
                r = slot_req[s * CAP + c]
                col = 8 * i + 2 * c
                factor = jnp.exp(stats[:, col : col + 1] - top[r])
                total[r] += stats[:, col + 1 : col + 2] * factor
                acc[r] += ret[s, c * rows : (c + 1) * rows, :] * factor


def merge(me, slot_req, ret, here):
    n = ret.shape[0]
    batch = min(16, n)
    one = jax.ShapeDtypeStruct(here[0].shape, F32)
    return pl.pallas_call(
        merge_kernel,
        out_shape=(one, one, one),
        in_specs=[SMEM, SMEM] + [VMEM] * 4,
        out_specs=(VMEM, VMEM, VMEM),
        scratch_shapes=[pltpu.VMEM((n // batch, BLK, batch * 8), F32)],
        compiler_params=params(),
        cost_estimate=cost(2),
        name="merge",
    )(me, slot_req, ret, *here)


def final_kernel(flags, acc, top, total, p0, p1, p2, p3, out, past):
    req, rows, _ = acc.shape
    part = req * rows
    tiles = part // BLK
    per = BLK // rows
    parts = (p0, p1, p2, p3)
    past[...] = jnp.concatenate([p[part:, :] for p in parts], axis=0).T
    for r in range(req):
        use = flags[r] == 1
        at = (r % per) * rows
        tops, sums = [], []
        for p in range(XS):
            col = (p * tiles + r // per) * 8
            stat = past[at : at + rows, col : col + 2]
            tops.append(jnp.where(use, stat[:, 0:1], NEG))
            sums.append(stat[:, 1:2])
        peak = top[r]
        for found in tops:
            peak = jnp.maximum(peak, found)
        factor = jnp.exp(top[r] - peak)
        sum_l, sum_o = total[r] * factor, acc[r] * factor
        for p in range(XS):
            factor = jnp.exp(tops[p] - peak)
            sum_l = sum_l + sums[p] * factor
            sum_o = sum_o + parts[p][r * rows : (r + 1) * rows, :] * factor
        out[r] = (sum_o / sum_l).astype(BF16)


def final(flags, merged, past):
    req, rows, _ = merged[0].shape
    return pl.pallas_call(
        final_kernel,
        out_shape=jax.ShapeDtypeStruct((req, rows, HD), BF16),
        in_specs=[SMEM] + [VMEM] * (3 + XS),
        out_specs=VMEM,
        scratch_shapes=[pltpu.VMEM((BLK, XS * (req * rows // BLK) * 8), F32)],
        compiler_params=params(),
        cost_estimate=cost(1),
        name="final",
    )(flags, *merged, *past)


def after(value, *others):
    return lax.optimization_barrier((value, others))[0]


def per_device(queries, new_kv, pool, page, lengths, outbox, prefix_store, owner, flags):
    req, steps, width = queries.shape
    pool_size = pool.shape[0]
    rows = steps * (width // HD)
    n = lax.axis_size("inst")
    shares = lax.axis_size("tp")
    ys = n // (XS * ZS)
    plane = ys * ZS
    me = lax.axis_index("inst").astype(jnp.int32)
    owned = owner[0]

    def index(y, x, z):
        return ((y % ys) * XS + x % XS) * ZS + z % ZS

    def move(value, dy, dx, dz):
        pairs = [
            (index(y, x, z), index(y + dy, x + dx, z + dz))
            for y in range(ys)
            for x in range(XS)
            for z in range(ZS)
        ]
        return lax.ppermute(value, "inst", pairs)

    steps_out = (
        (3, 0, 0, 0),
        (3, 0, 0, 1),
        (3, 0, 1, 0),
        (3, 0, -1, 0),
        (2, 1, 0, 0),
        (2, -1, 0, 0),
    )
    parts = []
    first = 0
    for units, _, _, _ in steps_out:
        parts.append(prefix_store[:, first * HD : (first + units) * HD] if first else None)
        first += units
    columns = [after(prefix_store, *parts[1:])[:, : steps_out[0][0] * HD]]
    holders = [owned]
    for part, (_, dy, dx, dz) in zip(parts[1:], steps_out[1:]):
        columns.append(move(part, dy, dx, dz))
        holders.append(index(owned // (XS * ZS) + dy, owned // ZS + dx, owned + dz))
    hold = sum(jnp.where(me == holders[k], k, 0) for k in range(1, len(steps_out)))
    spots = [
        ((i // ZS) % XS) * plane + (i // (XS * ZS)) * ZS + i % ZS for i in range(n)
    ]

    q = queries.reshape(req, rows, HD)
    local, slot_req, counts = prep(page, lengths, pool_size, n * CAP)
    tokens = prefix_store.shape[0] // n
    tokens = prefix_store.shape[0] // n
    units = tuple(step[0] for step in steps_out)
    pay = pack(spots, slot_req, counts, hold.reshape(1), q, columns)
    asked = lax.all_to_all(pay, "inst", split_axis=0, concat_axis=0, tiled=True)
    fresh = jnp.pad(new_kv, ((0, 0), (0, 16 - steps), (0, 0)))
    here = local_partials(local, pool, q, fresh)

    cores = 2
    chips = shares // cores
    core = lax.axis_index("tp").astype(jnp.int32) % cores
    mine, other = gather(
        units, core.reshape(1), jnp.stack(holders).astype(jnp.int32), asked, tokens
    )
    other = lax.ppermute(after(other, *here), "tp", [(t, t ^ 1) for t in range(shares)])
    both = jnp.stack([mine, other], axis=1)
    sheets = [
        [
            index(y + (ys // 2) * c, x, z) * shares + chip_of(p, c, chips) * cores + c
            for y in range(ys)
            for p in range(chips)
            for z in range(ZS)
        ]
        for x in range(XS)
        for c in range(cores)
    ]
    flat = after(q.reshape(req * rows, HD), both)
    guests = [flat] + [move(flat, 0, s, 0) for s in range(1, XS)]
    whole = (ys, chips, ZS) + both.shape[1:]
    spread = jnp.broadcast_to(both[None, :, None], whole)
    prefix = lax.all_to_all(
        spread.reshape((-1,) + both.shape[1:]),
        ("inst", "tp"),
        split_axis=0,
        concat_axis=0,
        tiled=True,
        axis_index_groups=sheets,
    ).reshape(whole)
    ret = remote_partials(outbox.reshape(-1), pool, asked, rows)
    back = lax.all_to_all(after(ret, prefix, *guests), "inst", split_axis=0, concat_axis=0, tiled=True)
    past = prefix_partials(guests[1:], prefix)
    sent = [move(past[s - 1], 0, -s, 0) for s in range(1, XS)]
    own = prefix_partials([after(flat, past[0])], prefix)
    past = [own[0]] + sent
    merged = merge(me.reshape(1), slot_req, back, here)
    out = final(flags, merged, past)
    return out.reshape(req, steps, width)


def solution(mesh):
    placed = (
        P("inst", None, "tp"),
        P("inst", None, "tp"),
        P("inst", None, "tp"),
        P("inst", None),
        P("inst"),
        P("inst", None, None),
        P(("inst", "tp"), None),
        P(),
        P("inst"),
    )
    return jax.shard_map(
        per_device, mesh=mesh, in_specs=placed, out_specs=P("inst", None, "tp"), check_vma=False
    )
```

```python
import functools

import jax
import jax.numpy as jnp
from jax import lax
from jax.experimental import pallas as pl
from jax.experimental.pallas import tpu as pltpu
from jax.sharding import PartitionSpec as P

HD = 128
BLK = 128
CAP = 2
KEPT = 16
NEG = -1e30
XS = 4
ZS = 2
F32 = jnp.float32
BF16 = jnp.bfloat16

VMEM = pl.BlockSpec(memory_space=pltpu.VMEM)
SMEM = pl.BlockSpec(memory_space=pltpu.SMEM)


def params():
    return pltpu.CompilerParams(vmem_limit_bytes=8 * 1024 * 1024)


def cost(us):
    return pl.CostEstimate(flops=0, bytes_accessed=int(us * 3.0e6), transcendentals=0)


def dot_nt(a, b):
    return lax.dot_general(a, b, (((1,), (1,)), ((), ())), preferred_element_type=F32)


def dot_nn(a, b):
    return lax.dot_general(a, b, (((1,), (0,)), ((), ())), preferred_element_type=F32)


def with_ones(values):
    return jnp.concatenate([values, jnp.ones_like(values)], axis=1)


def batch_partials(jobs):
    rows = jobs[0][0].shape[0]
    scores = jnp.concatenate([dot_nt(q, keys) for q, keys, _, _ in jobs], axis=0) * (HD ** -0.5)
    masked = jobs[0][3] is not None
    if masked:
        valid = jnp.concatenate([job[3] for job in jobs], axis=0)
        scores = jnp.where(valid, scores, NEG)
    top = jnp.max(scores, axis=-1, keepdims=True)
    weights = jnp.exp(scores - top)
    if masked:
        weights = jnp.where(valid, weights, 0.0)
    weights = weights.astype(BF16)
    found = []
    for i, (_, _, values, _) in enumerate(jobs):
        both = dot_nn(weights[i * rows : (i + 1) * rows], with_ones(values))
        found.append((top[i * rows : (i + 1) * rows], both[:, HD:], both[:, :HD]))
    return found


def prep_kernel(pool_size, page, lens, local, slot_req, counts):
    for k in range(KEPT):
        for field in range(3):
            local[field, k] = 0

    def request(r, kept):
        length = lens[r]

        def block(j, kept):
            b = page[r, j]
            valid = jnp.minimum(length - j * BLK, BLK)
            away = b >= pool_size

            @pl.when(away)
            def _():
                slot_req[b - pool_size] = r
                counts[b - pool_size] = valid

            @pl.when(jnp.logical_not(away))
            def _():
                local[0, kept] = b
                local[1, kept] = r
                local[2, kept] = valid

            return kept + jnp.where(away, 0, 1)

        return lax.fori_loop(0, lax.shift_right_logical(length + BLK - 1, 7), block, kept)

    lax.fori_loop(0, lens.shape[0], request, 0)


def prep(page, lengths, pool_size, slots):
    return pl.pallas_call(
        functools.partial(prep_kernel, pool_size),
        out_shape=(
            jax.ShapeDtypeStruct((3, KEPT), jnp.int32),
            jax.ShapeDtypeStruct((slots,), jnp.int32),
            jax.ShapeDtypeStruct((slots,), jnp.int32),
        ),
        in_specs=[SMEM, SMEM],
        out_specs=(SMEM, SMEM, SMEM),
        compiler_params=params(),
        cost_estimate=cost(3),
        name="prep",
    )(page, lengths)


def pack_kernel(spots, slot_req, counts, hold, q, *refs):
    sources, (pay, made, sems) = refs[:-3], refs[-3:]
    rows = q.shape[1]
    body = CAP * rows
    upper = lax.broadcasted_iota(jnp.int32, (16, HD), 0) < 8
    tokens = sources[0].shape[0] // len(spots)
    most = sources[0].shape[1] // HD
    groups = sems.shape[0]
    each = len(spots) // groups
    copies = []
    for g in range(groups):
        members = range(g * each, (g + 1) * each)
        for d in members:
            for c in range(CAP):
                made[d, c * rows : (c + 1) * rows, :] = q[slot_req[CAP * d + c]]
            tile = jnp.where(upper, counts[CAP * d], counts[CAP * d + 1])
            made[d, body : body + 16, :] = tile.astype(F32).astype(BF16)
        for k, source in enumerate(sources):

            @pl.when(hold[0] == k)
            def _():
                for d in members:
                    for j in range(most):
                        at = body + 16 + j * tokens
                        col = (j % (source.shape[1] // HD)) * HD
                        made[d, at : at + tokens, :] = source[
                            spots[d] * tokens : (spots[d] + 1) * tokens, col : col + HD
                        ]

        part = pl.ds(g * each, each)
        copies.append(pltpu.make_async_copy(made.at[part], pay.at[part], sems.at[g]))
        copies[-1].start()
    for copy in copies:
        copy.wait()


def pack(spots, slot_req, counts, hold, q, columns):
    n = len(spots)
    rows = q.shape[1]
    held, wide = columns[0].shape
    shape = (n, CAP * rows + 16 + (wide // HD) * (held // n), HD)
    return pl.pallas_call(
        functools.partial(pack_kernel, spots),
        out_shape=jax.ShapeDtypeStruct(shape, BF16),
        in_specs=[SMEM, SMEM, SMEM, VMEM] + [VMEM] * len(columns),
        out_specs=pl.BlockSpec(memory_space=pl.ANY),
        scratch_shapes=[pltpu.VMEM(shape, BF16), pltpu.SemaphoreType.DMA((4,))],
        compiler_params=params(),
        cost_estimate=cost(1.5),
        name="pack",
    )(slot_req, counts, hold, q, *columns)


def chip_of(position, core, chips):
    return (position + (chips // 2) * core) % chips


def gather_kernel(units, core, holders, asked, mine, other):
    chips, double, _ = mine.shape
    tokens = double // 2
    head = asked.shape[1] - units[0] * tokens
    found = [(k, j) for k, count in enumerate(units) for j in range(count)]
    for c in range(2):

        @pl.when(core[0] == c)
        def _():
            for out, parity in ((mine, c), (other, 1 - c)):
                for position in range(chips):
                    for part in range(2):
                        k, j = found[(chip_of(position, parity, chips) * 2 + parity) * 2 + part]
                        at = head + j * tokens
                        out[position, part * tokens : (part + 1) * tokens, :] = asked[
                            holders[k], at : at + tokens, :
                        ]


def gather(units, core, holders, asked, tokens):
    one = jax.ShapeDtypeStruct((sum(units) // 4, 2 * tokens, HD), BF16)
    return pl.pallas_call(
        functools.partial(gather_kernel, units),
        out_shape=(one, one),
        in_specs=[SMEM, SMEM, VMEM],
        out_specs=(VMEM, VMEM),
        compiler_params=params(),
        cost_estimate=cost(0.5),
        name="gather",
    )(core, holders, asked)


def remote_kernel(outbox, pool, pay, back, ret, sems):
    n = pay.shape[0]
    rows = (ret.shape[1] - 8) // CAP
    each = BLK // rows
    lane = lax.broadcasted_iota(jnp.int32, (rows, BLK), 1)

    def group(g, carry):
        jobs = []
        for i in range(each):
            d = g * each + i
            marks = pay[d, CAP * rows : CAP * rows + 16, :].astype(F32).astype(jnp.int32)
            for c in range(CAP):
                kv = pool[outbox[d * CAP + c]]
                valid = lane < marks[8 * c : 8 * c + 1, :]
                jobs.append((pay[d, c * rows : (c + 1) * rows, :], kv[:, :HD], kv[:, HD:], valid))
        found = batch_partials(jobs)
        stats = []
        for i in range(each):
            stat = jnp.zeros((rows, BLK), F32)
            for c in range(CAP):
                top, total, out = found[i * CAP + c]
                ret[g * each + i, c * rows : (c + 1) * rows, :] = out
                stat = jnp.where(lane == 2 * c, top, stat)
                stat = jnp.where(lane == 2 * c + 1, total, stat)
            stats.append(stat)
        turned = jnp.concatenate(stats, axis=0).T[:8]
        for i in range(each):
            ret[g * each + i, CAP * rows : CAP * rows + 8, :] = turned
        leave(g).start()
        return carry

    def leave(g):
        part = pl.ds(g * each, each)
        return pltpu.make_async_copy(ret.at[part], back.at[part], sems.at[g])

    def left(g, carry):
        leave(g).wait()
        return carry

    lax.fori_loop(0, n // each, group, 0)
    lax.fori_loop(0, n // each, left, 0)


def remote_partials(outbox, pool, pay, rows):
    n = pay.shape[0]
    shape = (n, CAP * rows + 8, HD)
    return pl.pallas_call(
        remote_kernel,
        out_shape=jax.ShapeDtypeStruct(shape, F32),
        in_specs=[SMEM, VMEM, VMEM],
        out_specs=pl.BlockSpec(memory_space=pl.ANY),
        scratch_shapes=[pltpu.VMEM(shape, F32), pltpu.SemaphoreType.DMA((n * rows // BLK,))],
        compiler_params=params(),
        cost_estimate=cost(6),
        name="remote_partials",
    )(outbox, pool, pay)


def local_kernel(local, pool, q, fresh, out_o, out_m, out_l):
    req, rows, _ = q.shape
    steps = rows // 8
    keys = fresh.shape[1]
    step = lax.broadcasted_iota(jnp.int32, (rows, keys), 0) // 8
    place = lax.broadcasted_iota(jnp.int32, (rows, keys), 1)
    causal = (place <= step) & (place < steps)
    found = batch_partials([(q[r], fresh[r, :, :HD], fresh[r, :, HD:], causal) for r in range(req)])
    for r, (top, total, out) in enumerate(found):
        out_o[r] = out
        out_l[r] = total
        out_m[r] = jnp.broadcast_to(top, (rows, HD))
    lane = lax.broadcasted_iota(jnp.int32, (rows, BLK), 1)

    def batch(g, carry):
        jobs = []
        for i in range(8):
            k = g * 8 + i
            kv = pool[local[0, k]]
            jobs.append((q[local[1, k]], kv[:, :HD], kv[:, HD:], lane < local[2, k]))
        found = batch_partials(jobs)
        for i in range(8):
            r = local[1, g * 8 + i]
            top, total, out = found[i]
            old = out_m[r]
            new = jnp.maximum(old, top)
            keep, add = jnp.exp(old - new), jnp.exp(top - new)
            out_m[r] = new
            out_l[r] = out_l[r] * keep + total * add
            out_o[r] = out_o[r] * keep + out * add
        return carry

    lax.fori_loop(0, KEPT // 8, batch, 0)


def local_partials(local, pool, q, fresh):
    one = jax.ShapeDtypeStruct(q.shape, F32)
    return pl.pallas_call(
        local_kernel,
        out_shape=(one, one, one),
        in_specs=[SMEM, VMEM, VMEM, VMEM],
        out_specs=(VMEM, VMEM, VMEM),
        compiler_params=params(),
        cost_estimate=cost(6),
        name="local_partials",
    )(local, pool, q, fresh)


def prefix_kernel(count, *refs):
    sources, kv, targets = refs[:count], refs[count], refs[count + 1 : 2 * count + 1]
    q, out_o, out_m, out_l = refs[2 * count + 1 :]
    chips, cores, double = kv.shape[1], kv.shape[3], kv.shape[4]
    tokens = double // 2
    part = sources[0].shape[0]
    for s, source in enumerate(sources):
        q[s * part : (s + 1) * part, :] = source[...]
    out_o[...] = jnp.zeros_like(out_o)
    out_l[...] = jnp.zeros_like(out_l)
    out_m[...] = jnp.full_like(out_m, NEG)

    def pair(t, carry):
        jobs = []
        for b in range(cores):
            keys = kv[:, t, :, b, :tokens].reshape(BLK, HD)
            values = kv[:, t, :, b, tokens:].reshape(BLK, HD)
            jobs.append((q[...], keys, values, None))
        found = batch_partials(jobs)
        old = out_m[...]
        new = jnp.maximum(jnp.maximum(old, found[0][0]), found[1][0])
        keep = jnp.exp(old - new)
        acc_l, acc_o = out_l[...] * keep, out_o[...] * keep
        for top, total, out in found:
            add = jnp.exp(top - new)
            acc_l = acc_l + total * add
            acc_o = acc_o + out * add
        out_m[...] = new
        out_l[...] = acc_l
        out_o[...] = acc_o
        return carry

    lax.fori_loop(0, chips, pair, 0)
    lane = lax.broadcasted_iota(jnp.int32, (BLK, HD), 1)
    for s, target in enumerate(targets):
        target[:part, :] = out_o[s * part : (s + 1) * part, :]
        for k in range(part // BLK):
            at = s * part + k * BLK
            stat = jnp.where(lane == 0, out_m[at : at + BLK, :], out_l[at : at + BLK, :])
            target[part + 8 * k : part + 8 * k + 8, :] = stat.T[:8]


def prefix_partials(queries, kv):
    part = queries[0].shape[0]
    one = jax.ShapeDtypeStruct((part + 8 * (part // BLK), HD), F32)
    whole = pltpu.VMEM((len(queries) * part, HD), F32)
    return pl.pallas_call(
        functools.partial(prefix_kernel, len(queries)),
        out_shape=(one,) * len(queries),
        in_specs=[VMEM] * (len(queries) + 1),
        out_specs=(VMEM,) * len(queries),
        scratch_shapes=[pltpu.VMEM((len(queries) * part, HD), BF16), whole, whole, whole],
        compiler_params=params(),
        cost_estimate=cost(len(queries)),
        name="prefix_partials",
    )(*queries, kv)


def merge_kernel(me, slot_req, ret, lo, lm, ll, acc, top, total, turned):
    req, rows, _ = lo.shape
    n = ret.shape[0]
    batch = min(16, n)
    body = CAP * rows
    per = BLK // rows
    for g in range(n // batch):
        turned[g] = ret[g * batch : (g + 1) * batch, body : body + 8, :].reshape(batch * 8, BLK).T
    mine = pl.multiple_of(lax.rem(me[0], per) * rows, rows)
    top[...] = lm[...]
    for g in range(n // batch):
        stats = turned[g, pl.ds(mine, rows), :]
        for i in range(batch):
            for c in range(CAP):
                r = slot_req[(g * batch + i) * CAP + c]
                col = 8 * i + 2 * c
                top[r] = jnp.maximum(top[r], stats[:, col : col + 1])
    for r in range(req):
        factor = jnp.exp(lm[r] - top[r])
        total[r] = ll[r] * factor
        acc[r] = lo[r] * factor
    for g in range(n // batch):
        stats = turned[g, pl.ds(mine, rows), :]
        for i in range(batch):
            for c in range(CAP):
                s = g * batch + i
                r = slot_req[s * CAP + c]
                col = 8 * i + 2 * c
                factor = jnp.exp(stats[:, col : col + 1] - top[r])
                total[r] += stats[:, col + 1 : col + 2] * factor
                acc[r] += ret[s, c * rows : (c + 1) * rows, :] * factor


def merge(me, slot_req, ret, here):
    n = ret.shape[0]
    batch = min(16, n)
    one = jax.ShapeDtypeStruct(here[0].shape, F32)
    return pl.pallas_call(
        merge_kernel,
        out_shape=(one, one, one),
        in_specs=[SMEM, SMEM] + [VMEM] * 4,
        out_specs=(VMEM, VMEM, VMEM),
        scratch_shapes=[pltpu.VMEM((n // batch, BLK, batch * 8), F32)],
        compiler_params=params(),
        cost_estimate=cost(2),
        name="merge",
    )(me, slot_req, ret, *here)


def final_kernel(flags, acc, top, total, p0, p1, p2, p3, out, past):
    req, rows, _ = acc.shape
    part = req * rows
    tiles = part // BLK
    per = BLK // rows
    parts = (p0, p1, p2, p3)
    past[...] = jnp.concatenate([p[part:, :] for p in parts], axis=0).T
    for r in range(req):
        use = flags[r] == 1
        at = (r % per) * rows
        tops, sums = [], []
        for p in range(XS):
            col = (p * tiles + r // per) * 8
            stat = past[at : at + rows, col : col + 2]
            tops.append(jnp.where(use, stat[:, 0:1], NEG))
            sums.append(stat[:, 1:2])
        peak = top[r]
        for found in tops:
            peak = jnp.maximum(peak, found)
        factor = jnp.exp(top[r] - peak)
        sum_l, sum_o = total[r] * factor, acc[r] * factor
        for p in range(XS):
            factor = jnp.exp(tops[p] - peak)
            sum_l = sum_l + sums[p] * factor
            sum_o = sum_o + parts[p][r * rows : (r + 1) * rows, :] * factor
        out[r] = (sum_o / sum_l).astype(BF16)


def final(flags, merged, past):
    req, rows, _ = merged[0].shape
    return pl.pallas_call(
        final_kernel,
        out_shape=jax.ShapeDtypeStruct((req, rows, HD), BF16),
        in_specs=[SMEM] + [VMEM] * (3 + XS),
        out_specs=VMEM,
        scratch_shapes=[pltpu.VMEM((BLK, XS * (req * rows // BLK) * 8), F32)],
        compiler_params=params(),
        cost_estimate=cost(1),
        name="final",
    )(flags, *merged, *past)


def after(value, *others):
    return lax.optimization_barrier((value, others))[0]


def per_device(queries, new_kv, pool, page, lengths, outbox, prefix_store, owner, flags):
    req, steps, width = queries.shape
    pool_size = pool.shape[0]
    rows = steps * (width // HD)
    n = lax.axis_size("inst")
    shares = lax.axis_size("tp")
    ys = n // (XS * ZS)
    plane = ys * ZS
    me = lax.axis_index("inst").astype(jnp.int32)
    owned = owner[0]

    def index(y, x, z):
        return ((y % ys) * XS + x % XS) * ZS + z % ZS

    def move(value, dy, dx, dz):
        pairs = [
            (index(y, x, z), index(y + dy, x + dx, z + dz))
            for y in range(ys)
            for x in range(XS)
            for z in range(ZS)
        ]
        return lax.ppermute(value, "inst", pairs)

    steps_out = (
        (3, 0, 0, 0),
        (3, 0, 0, 1),
        (3, 0, 1, 0),
        (3, 0, -1, 0),
        (2, 1, 0, 0),
        (2, -1, 0, 0),
    )
    parts = []
    first = 0
    for units, _, _, _ in steps_out:
        parts.append(prefix_store[:, first * HD : (first + units) * HD] if first else None)
        first += units
    columns = [after(prefix_store, *parts[1:])[:, : steps_out[0][0] * HD]]
    holders = [owned]
    for part, (_, dy, dx, dz) in zip(parts[1:], steps_out[1:]):
        columns.append(move(part, dy, dx, dz))
        holders.append(index(owned // (XS * ZS) + dy, owned // ZS + dx, owned + dz))
    hold = sum(jnp.where(me == holders[k], k, 0) for k in range(1, len(steps_out)))
    spots = [
        ((i // ZS) % XS) * plane + (i // (XS * ZS)) * ZS + i % ZS for i in range(n)
    ]

    q = queries.reshape(req, rows, HD)
    local, slot_req, counts = prep(page, lengths, pool_size, n * CAP)
    tokens = prefix_store.shape[0] // n
    tokens = prefix_store.shape[0] // n
    units = tuple(step[0] for step in steps_out)
    pay = pack(spots, slot_req, counts, hold.reshape(1), q, columns)
    asked = lax.all_to_all(pay, "inst", split_axis=0, concat_axis=0, tiled=True)
    fresh = jnp.pad(new_kv, ((0, 0), (0, 16 - steps), (0, 0)))
    here = local_partials(local, pool, q, fresh)

    cores = 2
    chips = shares // cores
    core = lax.axis_index("tp").astype(jnp.int32) % cores
    mine, other = gather(
        units, core.reshape(1), jnp.stack(holders).astype(jnp.int32), asked, tokens
    )
    other = lax.ppermute(after(other, *here), "tp", [(t, t ^ 1) for t in range(shares)])
    both = jnp.stack([mine, other], axis=1)
    sheets = [
        [
            index(y + (ys // 2) * c, x, z) * shares + chip_of(p, c, chips) * cores + c
            for y in range(ys)
            for p in range(chips)
            for z in range(ZS)
        ]
        for x in range(XS)
        for c in range(cores)
    ]
    flat = after(q.reshape(req * rows, HD), both)
    guests = [flat] + [move(flat, 0, s, 0) for s in range(1, XS)]
    whole = (ys, chips, ZS) + both.shape[1:]
    spread = jnp.broadcast_to(both[None, :, None], whole)
    prefix = lax.all_to_all(
        spread.reshape((-1,) + both.shape[1:]),
        ("inst", "tp"),
        split_axis=0,
        concat_axis=0,
        tiled=True,
        axis_index_groups=sheets,
    ).reshape(whole)
    ret = remote_partials(outbox.reshape(-1), pool, asked, rows)
    back = lax.all_to_all(after(ret, prefix, *guests), "inst", split_axis=0, concat_axis=0, tiled=True)
    past = prefix_partials(guests[1:], prefix)
    sent = [move(past[s - 1], 0, -s, 0) for s in range(1, XS)]
    own = prefix_partials([after(flat, past[0])], prefix)
    past = [own[0]] + sent
    merged = merge(me.reshape(1), slot_req, back, here)
    out = final(flags, merged, past)
    return out.reshape(req, steps, width)


def solution(mesh):
    placed = (
        P("inst", None, "tp"),
        P("inst", None, "tp"),
        P("inst", None, "tp"),
        P("inst", None),
        P("inst"),
        P("inst", None, None),
        P(("inst", "tp"), None),
        P(),
        P("inst"),
    )
    return jax.shard_map(
        per_device, mesh=mesh, in_specs=placed, out_specs=P("inst", None, "tp"), check_vma=False
    )
```
